32 devices in a mesh: body: 2 (over core), gx: 4 (over y, x), gy: 4 (over z).
Axes of the slice: x: 2, y: 2, z: 4, core: 2. Of those that a mesh axis runs over, the one named last changes fastest.
Arguments:
- surface_disp: float32 [2, 3, 49, 8192], P('body', None, None, ('gx', 'gy')), may hold values from -6 to 6
- proj_coords: float32 [2, 2, 36, 4096], P('body', None, None, ('gx', 'gy')), may hold values from -1 to 1
- pair_slave: int32 [2, 4096], P('body', ('gx', 'gy')), may hold values from 0 to 511
- pair_owner: int32 [2, 4096, 1], P('body', ('gx', 'gy')), may hold values from 0 to 15; in each aligned block of 256 rows (0 to 255, 256 to 511, ..., all dimensions but the last counted through in order) at most 24 rows name the same one
- send_list: int32 [2, 16, 384], P(None, ('gx', 'gy')), may hold values from 0 to 511
Outputs:
- nodal_force: float32 [2, 3, 192, 1536], P('body', None, 'gx', 'gy')
The draws below stay inside these ranges and needn't reach their ends.
Inputs may be any that keep to these rules, and one draw needn't show every extreme that they name: `pair_owner`: within the 256 pairs of one slave tile, at most 24 name the same owner tile; in some tile exactly 24 do.
All inputs are finite; a program needn't handle non-finite values.
Results may differ from the reference program's by a relative error of at most 0.0003.
Values sent between devices are 32-bit elements; how exact they have to be, the bound alone decides.
A program may use at most 64 MiB of HBM per device.

```python
import math
import jax
import jax.numpy as jnp
import numpy as np
from jax import lax

SX = 8
SY = 64
PAIR_DEV = 256
SEG_DEV = 512
CAP = 24
TILES = 16
SEGS = 8192
PAIRS = 4096
N_GX = 4
N_GY = 4


def plant(array, own_key, smallest, top_value):
    index_at = [jax.random.randint(jax.random.fold_in(own_key, axis), (), 0, length) for axis, length in enumerate(array.shape)]
    main_axis = array.shape.index(max(array.shape))
    next_to = index_at[:main_axis] + [(index_at[main_axis] + 1) % array.shape[main_axis]] + index_at[main_axis + 1:]
    return array.at[tuple(index_at)].set(smallest).at[tuple(next_to)].set(top_value)


def block_levels(own_key, extent, cuts, least, high):
    factor_of = 1.0
    for dim, shards_of in cuts:
        steps = jax.random.uniform(jax.random.fold_in(jax.random.fold_in(own_key, 6), dim), (shards_of,), jnp.float32, least / len(cuts), high / len(cuts))
        factor_of = factor_of * jnp.repeat(jnp.exp(steps), extent[dim] // shards_of).reshape((-1,) + (1,) * (len(extent) - 1 - dim))
    return factor_of


def assign_block(own_key, own, number, rows, number_of, top, limit, lean):
    order = jax.random.permutation(own_key, number_of)
    crowded, common = load_shares(number_of, rows * top, limit, lean, True), load_shares(number_of, rows * top, limit, lean, False)
    places = jnp.arange(number_of)

    def named(tallies, offset_by):
        used = int((tallies > 0).sum())
        fixed = max(1, used // 4)
        passed = fixed + (places - fixed + offset_by * (used - fixed)) % max(1, number_of - fixed)
        return jnp.zeros((number_of,), jnp.int32).at[order[jnp.where(places < fixed, places, passed)]].set(jnp.asarray(tallies, jnp.int32))

    tallies = jnp.where(number % 4 == 0, named(crowded, number // 4), named(common, number - number // 4 - 1))
    mixed = jax.random.permutation(jax.random.fold_in(own, 3), number_of)
    source_of, taker = mixed[0:number_of // 2 * 2:2], mixed[1:number_of // 2 * 2:2]
    margin = jnp.minimum(tallies[source_of] - 1, limit - tallies[taker]) // 2
    margin = jnp.where((source_of == order[0]) | (taker == order[0]) | (tallies[taker] == 0), 0, jnp.maximum(margin, 0))
    passed = jax.random.randint(jax.random.fold_in(own, 4), (number_of // 2,), 0, 1 << 20) % (margin + 1)
    tallies = tallies.at[source_of].add(-passed).at[taker].add(passed)
    labels = jnp.searchsorted(jnp.cumsum(tallies), jnp.arange(rows * top), side="right").astype(jnp.int32)
    table = labels.reshape(top, rows).T
    table = table[jax.random.permutation(jax.random.fold_in(own, 1), rows)]
    offset_by = jax.random.randint(jax.random.fold_in(own, 2), (rows, 1), 0, top)
    return jnp.take_along_axis(table, (jnp.arange(top)[None, :] + offset_by) % top, axis=1)


def load_shares(number_of, total, limit, lean, full):
    weights = [(1 << 20) // math.isqrt(standing ** lean) + 1 for standing in range(1, number_of + 1)]
    largest = limit if full else min(limit, max(-(-total // number_of), total * weights[0] // sum(weights)))
    least = 1 if total - largest >= number_of - 1 else 0
    counts, spare = [largest] + [least] * (number_of - 1), total - largest - least * (number_of - 1)
    while spare > 0:
        movable = [i for i in range(1, number_of) if counts[i] < largest] or [i for i in range(1, number_of) if counts[i] < limit]
        pool, remaining = sum([weights[i] for i in movable]), spare
        for i in movable:
            extra = min(limit - counts[i], max(1, remaining * weights[i] // pool), spare)
            counts[i] = counts[i] + extra
            spare = spare - extra
    return np.array(counts)


def scatter_about(own_key, shape, width, most, split=(), kind=jnp.bfloat16):
    array = width * jax.random.normal(own_key, shape, jnp.float32)
    if split:
        array = array * block_levels(own_key, shape, split, -0.22, 0.18)
    return jnp.clip(array, -most, most).astype(kind)


def setup_inputs(seed: int = 0) -> dict:
    key_of = jax.random.split(jax.random.key(seed), 6)
    surface_disp = scatter_about(key_of[0], (2, 3, 49, SEGS), 1.0, 6.0, ((0, 2), (3, 16)), jnp.float32)
    proj_coords = jnp.clip(jax.random.uniform(key_of[1], (2, 2, 36, PAIRS), jnp.float32, -1.0, 1.0) * block_levels(key_of[1], (2, 2, 36, PAIRS), ((0, 2), (3, 16)), -0.4, 0.0), -1.0, 1.0)
    pair_slave = plant(jax.random.randint(key_of[2], (2, PAIRS), 0, SEG_DEV), jax.random.fold_in(key_of[2], 1), 0, SEG_DEV - 1).astype(jnp.int32)
    pair_owner_keys = jax.random.split(jax.random.fold_in(key_of[3], 1), 2 * PAIRS // PAIR_DEV)
    pair_owner_turns = jax.random.permutation(jax.random.fold_in(key_of[3], 3), 2 * PAIRS // PAIR_DEV)
    pair_owner = jax.vmap(lambda own, number: assign_block(jax.random.fold_in(key_of[3], 2), own, number, PAIR_DEV, TILES, 1, CAP, 2))(pair_owner_keys, pair_owner_turns).reshape((2, PAIRS, 1))
    send_list = plant(jax.random.randint(key_of[4], (2, TILES, TILES * CAP), 0, SEG_DEV), jax.random.fold_in(key_of[4], 1), 0, SEG_DEV - 1).astype(jnp.int32)
    return dict(surface_disp=surface_disp, proj_coords=proj_coords, pair_slave=pair_slave, pair_owner=pair_owner, send_list=send_list)


KAPPA = 2.0
SHEAR = 1.0
LOBATTO_POINTS = (-1.0, -0.8302238962785670, -0.4688487934707142, 0.0, 0.4688487934707142, 0.8302238962785670, 1.0)
GAUSS_POINTS = (-0.9324695142031521, -0.6612093864662645, -0.2386191860831969, 0.2386191860831969, 0.6612093864662645, 0.9324695142031521)
GAUSS_WEIGHTS = (0.1713244923791704, 0.3607615730481386, 0.4679139345726910, 0.4679139345726910, 0.3607615730481386, 0.1713244923791704)


def basis_traced(abscissa):
    points = LOBATTO_POINTS
    factors = []
    for k in range(7):
        product = jnp.ones_like(abscissa)
        for m in range(7):
            if m != k:
                product = product * ((abscissa - points[m]) * (1.0 / (points[k] - points[m])))
        factors.append(product)
    return jnp.stack(factors)


def slave_table():
    single = basis_traced(jnp.asarray(GAUSS_POINTS, jnp.float32)).T
    return (single[:, None, :, None] * single[None, :, None, :]).reshape(36, 49)


def quad_weights():
    weights = jnp.asarray(GAUSS_WEIGHTS, jnp.float32)
    return (weights[:, None] * weights[None, :]).reshape(36)


def pair_forces(slave_nodes, master_nodes, pair_coords, normal_sign):
    highest = lax.Precision.HIGHEST
    slave_basis = slave_table()
    quad_weight = quad_weights()
    first_basis = basis_traced(pair_coords[0])
    second_basis = basis_traced(pair_coords[1])
    slave_value = jnp.einsum("qi,cip->cqp", slave_basis, slave_nodes, precision=highest)
    master_grid = master_nodes.reshape(3, 7, 7, -1)
    partial_sum = jnp.einsum("lqp,cklp->ckqp", second_basis, master_grid, precision=highest)
    master_value = jnp.sum(first_basis[None] * partial_sum, axis=1)
    offset = master_value - slave_value
    normal_gap = normal_sign * offset[2]
    pressure = KAPPA * jax.nn.softplus(-normal_gap)
    traction = jnp.stack([SHEAR * offset[0], SHEAR * offset[1], -normal_sign * pressure]) * quad_weight[None, :, None]
    slave_force = jnp.einsum("qi,cqp->cip", slave_basis, traction, precision=highest)
    weighted = second_basis[None] * traction[:, None]
    master_force = -jnp.einsum("kqp,clqp->cklp", first_basis, weighted, precision=highest).reshape(3, 49, -1)
    return slave_force, master_force


def slot_ranks(owners, tile_count):
    onehot = (owners[:, None] == jnp.arange(tile_count, dtype=jnp.int32)[None, :]).astype(jnp.int32)
    before = jnp.cumsum(onehot, axis=0) - onehot
    return jnp.sum(before * onehot, axis=1).astype(jnp.int32)


def assemble_periodic(element_force):
    segment_grid = element_force.reshape(3, 7, 7, N_GX, N_GY, SX, SY)
    segment_grid = segment_grid.transpose(0, 1, 2, 3, 5, 4, 6).reshape(3, 7, 7, N_GX * SX, N_GY * SY)
    along_x = segment_grid[:, :6].at[:, 0].add(jnp.roll(segment_grid[:, 6], 1, axis=2))
    along_y = along_x[:, :, :6].at[:, :, 0].add(jnp.roll(along_x[:, :, 6], 1, axis=3))
    return along_y.transpose(0, 3, 1, 4, 2).reshape(3, 6 * N_GX * SX, 6 * N_GY * SY)


def reference(surface_disp, proj_coords, pair_slave, pair_owner, send_list):
    tile_count = N_GX * N_GY
    segment_count = SX * SY
    running = (jnp.zeros((3, 49, tile_count * segment_count), jnp.float32),
               jnp.zeros((3, 49, tile_count * segment_count), jnp.float32))
    for body_side in range(2):
        other_side = 1 - body_side
        normal_sign = 1.0 - 2.0 * body_side

        def per_tile(state, tile_index):
            start = tile_index * PAIR_DEV
            slaves = lax.dynamic_slice_in_dim(pair_slave[body_side], start, PAIR_DEV)
            owners = lax.dynamic_slice_in_dim(pair_owner[body_side, :, 0], start, PAIR_DEV)
            pair_coords = lax.dynamic_slice_in_dim(proj_coords[body_side], start, PAIR_DEV, axis=2)
            slot_rank = slot_ranks(owners, tile_count)
            masters = send_list[other_side][owners, tile_index * CAP + slot_rank]
            master_ids = (owners * segment_count + masters).astype(jnp.int32)
            slave_ids = (tile_index * segment_count + slaves).astype(jnp.int32)
            slave_nodes = jnp.take(surface_disp[body_side], slave_ids, axis=2)
            master_nodes = jnp.take(surface_disp[other_side], master_ids, axis=2)
            slave_force, master_force = pair_forces(slave_nodes, master_nodes, pair_coords, normal_sign)
            forces = list(state)
            forces[body_side] = forces[body_side].at[:, :, slave_ids].add(slave_force)
            forces[other_side] = forces[other_side].at[:, :, master_ids].add(master_force)
            return tuple(forces), None

        running, skipped = lax.scan(per_tile, running, jnp.arange(tile_count, dtype=jnp.int32))
    return jnp.stack([assemble_periodic(running[0]), assemble_periodic(running[1])])
```

```python
import functools

import jax
import jax.numpy as jnp
import numpy as np
from jax import lax
from jax.experimental import pallas as pl
from jax.experimental.pallas import tpu as pltpu
from jax.sharding import PartitionSpec as P

SX = 8
SY = 64
KAPPA = 2.0
SHEAR = 1.0
LOBATTO_POINTS = (
    -1.0,
    -0.830223896278567,
    -0.4688487934707142,
    0.0,
    0.4688487934707142,
    0.830223896278567,
    1.0,
)
GAUSS_POINTS = (
    -0.932469514203152,
    -0.6612093864662645,
    -0.2386191860831969,
    0.2386191860831969,
    0.6612093864662645,
    0.932469514203152,
)
GAUSS_WEIGHTS = (
    0.1713244923791704,
    0.3607615730481386,
    0.467913934572691,
    0.467913934572691,
    0.3607615730481386,
    0.1713244923791704,
)
MESH = pl.DeviceIdType.MESH
F32 = jnp.float32
BF16 = jnp.bfloat16
NODES = 49
VALUES = 3 * NODES
LANES = 128
TAIL = VALUES - LANES
STRIDE = LANES // 6
ROWS = 160
QUADS = 36
QPAD = 40
SCALE = tuple(
    1.0 / float(np.prod([LOBATTO_POINTS[k] - LOBATTO_POINTS[m] for m in range(7) if m != k]))
    for k in range(7)
)


def tables():
    gauss = np.array(GAUSS_POINTS)
    single = np.ones((6, 7))
    for k in range(7):
        for m in range(7):
            if m != k:
                single[:, k] *= (gauss - LOBATTO_POINTS[m]) / (LOBATTO_POINTS[k] - LOBATTO_POINTS[m])
    slave = (single[:, None, :, None] * single[None, :, None, :]).reshape(QUADS, NODES)
    spread = np.zeros((3 * QPAD, ROWS), np.float32)
    for c in range(3):
        spread[c * QPAD : c * QPAD + QUADS, c * NODES : (c + 1) * NODES] = slave
    weights = np.array(GAUSS_WEIGHTS)
    quad = np.zeros((QPAD, LANES), np.float32)
    quad[:QUADS] = (weights[:, None] * weights[None, :]).reshape(QUADS, 1)
    order = np.zeros((7 * 24, 2 * LANES), np.float32)
    for column in range(2 * LANES):
        place = column if column < LANES else LANES + (column - LANES) % STRIDE
        if place < VALUES and column < LANES + 6 * STRIDE:
            c, k, m = place // NODES, place % NODES // 7, place % 7
            m = (place % NODES) % 7
            order[m * 24 + c * 8 + k, column] = 1
    join = np.zeros((6 * SX + 8, 8 * SX), np.float32)
    for la in range(SX):
        for k in range(7):
            join[6 * la + k, 8 * la + k] = 1
    return spread, spread.T.copy(), quad, order, join


def two(x):
    high = x.astype(BF16)
    return high, (x - high.astype(F32)).astype(BF16)


def dot(a, b):
    return jnp.dot(a, b, preferred_element_type=F32)


def dot_t(a, b):
    return lax.dot_general(a, b, (((1,), (1,)), ((), ())), preferred_element_type=F32)


def flag(condition):
    return jnp.where(condition, 1.0, 0.0).astype(BF16)


def basis(x):
    gaps = [x - r for r in LOBATTO_POINTS]
    before = [None] * 7
    after = [None] * 7
    for k in range(1, 7):
        before[k] = gaps[0] if k == 1 else before[k - 1] * gaps[k - 1]
    for k in range(5, -1, -1):
        after[k] = gaps[6] if k == 5 else after[k + 1] * gaps[k + 1]
    out = []
    for k in range(7):
        if k == 0:
            product = after[0]
        elif k == 6:
            product = before[6]
        else:
            product = before[k] * after[k]
        out.append(product * SCALE[k])
    return out


def tail_mask(shape, part):
    lane = lax.broadcasted_iota(jnp.int32, shape, 2)
    row = lax.broadcasted_iota(jnp.int32, shape, 1)
    start = STRIDE * (2 * part + jnp.where(row >= 4, 1, 0))
    return (lane >= start) & (lane < start + STRIDE)


def pack(gathered, send, tiles, slots):
    send[:, :slots, :] = gathered[:, :LANES].reshape(tiles, slots, LANES)
    tail = gathered[:, LANES:].reshape(tiles, slots, LANES)
    for group in range(-(-slots // 24)):
        total = None
        for part in range(min(3, slots // 8 - 3 * group)):
            row = 8 * (3 * group + part)
            block = tail[:, row : row + 8, :]
            block = jnp.where(tail_mask(block.shape, part), block, 0.0)
            total = block if total is None else total + block
        row = slots + 4 * group
        send[:, row : row + 4, :] = total[:, :4, :] + total[:, 4:, :]


def unpack(recv, tiles, slots):
    main = recv[:, :slots, :].reshape(tiles * slots, LANES)
    blocks = []
    for group in range(-(-slots // 24)):
        row = slots + 4 * group
        four = recv[:, row : row + 4, :]
        eight = jnp.concatenate([four, four], axis=1)
        for part in range(min(3, slots // 8 - 3 * group)):
            blocks.append(jnp.where(tail_mask(eight.shape, part), eight, 0.0))
    tail = jnp.concatenate(blocks, axis=1).reshape(tiles * slots, LANES)
    return jnp.concatenate([main.T, tail.T], axis=0)


def kernel(
    sizes,
    surf, coords, slaves, owners, lists, spread, spread_t, quad, order, join,
    out,
    s6, e12, lb1, lb2, value, tract, nodes, f6, pads, halo_row, halo_col,
    send1, recv1, send2, recv2, row_in, col_in, corner_in,
    ss1, rs1, ss2, rs2, hs, hr,
):
    wx, wy, capacity, slots, pairs, segs = sizes
    tiles = wx * wy
    body, gx, gy = lax.axis_index("body"), lax.axis_index("gx"), lax.axis_index("gy")
    other = 1 - body
    tile = gx * wy + gy
    next_x, next_y = lax.rem(gx + 1, wx), lax.rem(gy + 1, wy)
    back_x, back_y = lax.rem(gx + wx - 1, wx), lax.rem(gy + wy - 1, wy)

    barrier = pltpu.get_barrier_semaphore()

    def greet(j, carry):
        to = lax.rem(tile + j, tiles)
        pl.semaphore_signal(
            barrier, inc=1, device_id=(other, to // wy, lax.rem(to, wy)), device_id_type=MESH
        )
        return carry

    lax.fori_loop(0, tiles, greet, 0)
    for place in ((back_x, gy), (gx, back_y), (back_x, back_y)):
        pl.semaphore_signal(barrier, inc=1, device_id=(body,) + place, device_id_type=MESH)

    s6[...] = jnp.zeros_like(s6)
    for c in range(3):
        s6[c * NODES : (c + 1) * NODES, :] = surf[c]
    tail = s6[LANES:VALUES, :]
    for copy in range(1, 6):
        s6[LANES + copy * STRIDE : LANES + copy * STRIDE + TAIL, :] = tail
    high, low = two(s6[...])

    own = jnp.where(body == 0, lists[0], lists[1])
    pick = own.shape[1]
    column = jnp.broadcast_to(own, (LANES, pick)).T
    lane = lax.broadcasted_iota(jnp.int32, (pick, LANES), 1)
    list_hot = jnp.concatenate(
        [flag(column == lane + LANES * j) for j in range(segs // LANES)], axis=1
    )
    pack(dot_t(list_hot, high) + dot_t(list_hot, low), send1, tiles, slots)

    pl.semaphore_wait(barrier, tiles + 3)

    def copy_of(send, recv, ss, rs, to, land):
        return pltpu.make_async_remote_copy(
            src_ref=send.at[to],
            dst_ref=recv.at[land],
            send_sem=ss.at[to],
            recv_sem=rs.at[land],
            device_id=(other, to // wy, lax.rem(to, wy)),
            device_id_type=MESH,
        )

    def start_all(send, recv, ss, rs):
        def body_of(j, carry):
            to = lax.rem(tile + j, tiles)
            copy_of(send, recv, ss, rs, to, tile).start()
            return carry

        lax.fori_loop(0, tiles, body_of, 0)

    def wait_all(send, recv, ss, rs, arrive):
        def body_of(j, carry):
            copy = copy_of(send, recv, ss, rs, j, j)
            if arrive:
                copy.wait_recv()
            else:
                copy.wait_send()
            return carry

        lax.fori_loop(0, tiles, body_of, 0)

    start_all(send1, recv1, ss1, rs1)

    tile_row = lax.broadcasted_iota(jnp.int32, (tiles, pairs), 0)
    same = flag(tile_row == owners[...])
    earlier = flag(
        lax.broadcasted_iota(jnp.int32, (pairs, pairs), 0)
        < lax.broadcasted_iota(jnp.int32, (pairs, pairs), 1)
    )
    before = dot(same, earlier)
    rank = jnp.sum(before * same.astype(F32), axis=0, keepdims=True).astype(jnp.int32)
    slot = owners[...] * slots + rank
    slot_hot = flag(lax.broadcasted_iota(jnp.int32, (tiles * slots, pairs), 0) == slot)
    slave_hot = flag(lax.broadcasted_iota(jnp.int32, (segs, pairs), 0) == slaves[...])

    table_high, table_low = two(spread[...])
    gathered = dot(high[:ROWS], slave_hot) + dot(low[:ROWS], slave_hot)
    g_high, g_low = two(gathered)
    value[...] = dot(table_high, g_high) + (dot(table_high, g_low) + dot(table_low, g_high))

    e12[...] = jnp.zeros_like(e12)
    e12[0, :QUADS, :] = coords[0]
    e12[1, :QUADS, :] = coords[1]
    for chunk in range(QPAD // 8):
        at = slice(8 * chunk, 8 * chunk + 8)
        for axis, store in ((0, lb1), (1, lb2)):
            for k, factor in enumerate(basis(e12[axis, at, :])):
                store[k, at, :] = factor

    wide = SY * 6 + LANES
    source = lax.broadcasted_iota(jnp.int32, (7 * SY, wide), 0)
    target = jnp.minimum(lax.broadcasted_iota(jnp.int32, (7 * SY, wide), 1), 6 * SY)
    step_m = source // SY
    weave = flag(target == 6 * (source - step_m * SY) + step_m)

    wait_all(send1, recv1, ss1, rs1, True)
    master = unpack(recv1, tiles, slots)
    m_high, m_low = two(master)
    paired = dot(m_high, slot_hot) + dot(m_low, slot_hot)
    nodes[:LANES, :] = paired[:LANES]
    value_tail = paired[LANES : LANES + TAIL]
    for copy in range(1, 6):
        first = LANES + copy * STRIDE
        value_tail = value_tail + paired[first : first + TAIL]
    nodes[LANES:VALUES, :] = value_tail

    sign = 1.0 - 2.0 * body.astype(F32)
    for block in range(pairs // LANES):
        across = slice(block * LANES, (block + 1) * LANES)
        for chunk in range(QPAD // 8):
            at = slice(8 * chunk, 8 * chunk + 8)
            first = [lb1[k, at, across] for k in range(7)]
            second = [lb2[k, at, across] for k in range(7)]
            weight = quad[at, :]
            for c in range(3):
                total = None
                for k in range(7):
                    inner = None
                    for m in range(7):
                        row = c * NODES + 7 * k + m
                        term = second[m] * nodes[row : row + 1, across]
                        inner = term if inner is None else inner + term
                    term = first[k] * inner
                    total = term if total is None else total + term
                place = slice(c * QPAD + 8 * chunk, c * QPAD + 8 * chunk + 8)
                offset = total - value[place, across]
                if c < 2:
                    force = SHEAR * offset
                else:
                    gap = -sign * offset
                    soft = jnp.maximum(gap, 0.0) + jnp.log1p(jnp.exp(-jnp.abs(gap)))
                    force = -sign * KAPPA * soft
                tract[place, across] = force * weight

    f6[...] = jnp.zeros_like(f6)
    for block in range(pairs // LANES):
        across = slice(block * LANES, (block + 1) * LANES)
        for c in range(3):
            minus = -tract[c * QPAD : (c + 1) * QPAD, across]
            for m in range(7):
                weighted = lb2[m, :, across] * minus
                for k in range(7):
                    row = c * NODES + 7 * k + m
                    f6[row : row + 1, across] = jnp.sum(
                        lb1[k, :, across] * weighted, axis=0, keepdims=True
                    )
    tail = f6[LANES:VALUES, :]
    for copy in range(1, 6):
        f6[LANES + copy * STRIDE : LANES + copy * STRIDE + TAIL, :] = tail
    f_high, f_low = two(f6[...])
    pack(dot_t(slot_hot, f_high) + dot_t(slot_hot, f_low), send2, tiles, slots)
    start_all(send2, recv2, ss2, rs2)

    t_high, t_low = two(tract[...])
    back_high, back_low = two(spread_t[...])
    slave_force = dot(back_high, t_high) + (dot(back_high, t_low) + dot(back_low, t_high))
    a_high, a_low = two(slave_force)
    s6[:ROWS, :] = dot_t(a_high, slave_hot) + dot_t(a_low, slave_hot)
    s6[ROWS:, :] = jnp.zeros((2 * LANES - ROWS, segs), F32)

    wait_all(send2, recv2, ss2, rs2, True)
    r_high, r_low = two(unpack(recv2, tiles, slots))
    element = s6[...] + (dot(r_high, list_hot) + dot(r_low, list_hot))
    e_high, e_low = two(element)
    arrange = order[...].astype(BF16)
    ordered = dot(arrange, e_high) + dot(arrange, e_low)
    for m in range(7):
        for c in range(3):
            for la in range(SX):
                pads[c, 8 * la : 8 * la + 8, m * SY : (m + 1) * SY] = ordered[
                    m * 24 + c * 8 : m * 24 + c * 8 + 8, la * SY : (la + 1) * SY
                ]
    together = join[...].astype(BF16)
    lanes = lax.broadcasted_iota(jnp.int32, (6 * SX + 8, LANES), 1)
    column = jnp.zeros((6 * SX + 8, LANES), F32)
    halo_row[...] = jnp.zeros_like(halo_row)
    for c in range(3):
        p_high, p_low = two(pads[c])
        x_high, x_low = two(dot(together, p_high) + dot(together, p_low))
        grid = dot(x_high, weave) + dot(x_low, weave)
        out[c] = grid[: 6 * SX, : 6 * SY]
        halo_row[c : c + 1, :] = grid[6 * SX : 6 * SX + 1, : 6 * SY]
        column = jnp.where(lanes == c, grid[:, 6 * SY :], column)
    halo_col[...] = column

    messages = [
        (halo_row, row_in, (next_x, gy)),
        (halo_col.at[pl.ds(0, 6 * SX)], col_in, (gx, next_y)),
        (halo_col.at[pl.ds(6 * SX, 8)], corner_in, (next_x, next_y)),
    ]
    copies = [
        pltpu.make_async_remote_copy(
            src_ref=src,
            dst_ref=dst,
            send_sem=hs.at[i],
            recv_sem=hr.at[i],
            device_id=(body,) + place,
            device_id_type=MESH,
        )
        for i, (src, dst, place) in enumerate(messages)
    ]
    for copy in copies:
        copy.start()
    wait_all(send1, recv1, ss1, rs1, False)
    wait_all(send2, recv2, ss2, rs2, False)
    for copy in copies:
        copy.wait_recv()
    first_row = lax.broadcasted_iota(jnp.int32, (8, LANES), 0) == 0
    for c in range(3):
        out[c, 0:1, :] = out[c, 0:1, :] + row_in[c : c + 1, :]
        wide_lanes = lax.broadcasted_iota(jnp.int32, (6 * SX, LANES), 1)
        edge = jnp.sum(jnp.where(wide_lanes == c, col_in[...], 0.0), axis=1, keepdims=True)
        out[c, :, :LANES] = out[c, :, :LANES] + jnp.where(wide_lanes == 0, edge, 0.0)
        corner = jnp.sum(
            jnp.where(lanes[:8] == c, corner_in[...], 0.0), axis=1, keepdims=True
        )
        out[c, :8, :LANES] = out[c, :8, :LANES] + jnp.where(
            first_row & (lanes[:8] == 0), corner, 0.0
        )
    for copy in copies:
        copy.wait_send()


def local(surface_disp, proj_coords, pair_slave, pair_owner, send_list):
    wx, wy = lax.axis_size("gx"), lax.axis_size("gy")
    tiles = wx * wy
    segs = surface_disp.shape[-1]
    pairs = proj_coords.shape[-1]
    capacity = send_list.shape[-1] // tiles
    slots = -(-capacity // 8) * 8
    lists = send_list
    if slots != capacity:
        lists = lists.reshape(2, 1, tiles, capacity)
        lists = jnp.pad(lists, ((0, 0), (0, 0), (0, 0), (0, slots - capacity)), constant_values=-1)
        lists = lists.reshape(2, 1, tiles * slots)
    block = slots + 4 * -(-slots // 24)
    spread, spread_t, quad, order, join = tables()
    sizes = (wx, wy, capacity, slots, pairs, segs)
    vmem = pl.BlockSpec(memory_space=pltpu.VMEM)
    buffer = pltpu.VMEM((tiles, block, LANES), F32)
    result = pl.pallas_call(
        functools.partial(kernel, sizes),
        out_shape=jax.ShapeDtypeStruct((3, 6 * SX, 6 * SY), F32),
        in_specs=[vmem] * 10,
        out_specs=vmem,
        scratch_shapes=[
            pltpu.VMEM((2 * LANES, segs), F32),
            pltpu.VMEM((2, QPAD, pairs), F32),
            pltpu.VMEM((7, QPAD, pairs), F32),
            pltpu.VMEM((7, QPAD, pairs), F32),
            pltpu.VMEM((3 * QPAD, pairs), F32),
            pltpu.VMEM((3 * QPAD, pairs), F32),
            pltpu.VMEM((ROWS, pairs), F32),
            pltpu.VMEM((2 * LANES, pairs), F32),
            pltpu.VMEM((3, 8 * SX, 7 * SY), F32),
            pltpu.VMEM((8, 6 * SY), F32),
            pltpu.VMEM((6 * SX + 8, LANES), F32),
            buffer,
            buffer,
            buffer,
            buffer,
            pltpu.VMEM((8, 6 * SY), F32),
            pltpu.VMEM((6 * SX, LANES), F32),
            pltpu.VMEM((8, LANES), F32),
            pltpu.SemaphoreType.DMA((tiles,)),
            pltpu.SemaphoreType.DMA((tiles,)),
            pltpu.SemaphoreType.DMA((tiles,)),
            pltpu.SemaphoreType.DMA((tiles,)),
            pltpu.SemaphoreType.DMA((3,)),
            pltpu.SemaphoreType.DMA((3,)),
        ],
        compiler_params=pltpu.CompilerParams(
            collective_id=0, has_side_effects=True, vmem_limit_bytes=48 * 1024 * 1024
        ),
    )(
        surface_disp[0],
        proj_coords[0],
        pair_slave,
        pair_owner.reshape(1, pairs),
        lists,
        spread,
        spread_t,
        quad,
        order,
        join,
    )
    return result[None]


def solution(mesh):
    return jax.shard_map(
        local,
        mesh=mesh,
        in_specs=(
            P("body", None, None, ("gx", "gy")),
            P("body", None, None, ("gx", "gy")),
            P("body", ("gx", "gy")),
            P("body", ("gx", "gy"), None),
            P(None, ("gx", "gy"), None),
        ),
        out_specs=P("body", None, "gx", "gy"),
        check_vma=False,
    )
```

```python
import functools

import jax
import jax.numpy as jnp
import numpy as np
from jax import lax
from jax.experimental import pallas as pl
from jax.experimental.pallas import tpu as pltpu
from jax.sharding import PartitionSpec as P

SX = 8
SY = 64
KAPPA = 2.0
SHEAR = 1.0
LOBATTO_POINTS = (
    -1.0,
    -0.830223896278567,
    -0.4688487934707142,
    0.0,
    0.4688487934707142,
    0.830223896278567,
    1.0,
)
GAUSS_POINTS = (
    -0.932469514203152,
    -0.6612093864662645,
    -0.2386191860831969,
    0.2386191860831969,
    0.6612093864662645,
    0.932469514203152,
)
GAUSS_WEIGHTS = (
    0.1713244923791704,
    0.3607615730481386,
    0.467913934572691,
    0.467913934572691,
    0.3607615730481386,
    0.1713244923791704,
)
MESH = pl.DeviceIdType.MESH
F32 = jnp.float32
BF16 = jnp.bfloat16
NODES = 49
NPAD = 56
LANES = 128
HEAD = 40
TAIL = NODES - HEAD
QUADS = 36
QPAD = 40
BLOCK = 10
SCALE = tuple(
    1.0 / float(np.prod([LOBATTO_POINTS[k] - LOBATTO_POINTS[m] for m in range(7) if m != k]))
    for k in range(7)
)


def tables():
    gauss = np.array(GAUSS_POINTS)
    single = np.ones((6, 7))
    for k in range(7):
        for m in range(7):
            if m != k:
                single[:, k] *= (gauss - LOBATTO_POINTS[m]) / (LOBATTO_POINTS[k] - LOBATTO_POINTS[m])
    spread = np.zeros((QPAD, NPAD), np.float32)
    spread[:QUADS, :NODES] = (single[:, None, :, None] * single[None, :, None, :]).reshape(
        QUADS, NODES
    )
    weights = np.array(GAUSS_WEIGHTS)
    quad = np.zeros((QPAD, LANES), np.float32)
    quad[:QUADS] = (weights[:, None] * weights[None, :]).reshape(QUADS, 1)
    tile = np.zeros((LANES, 16), np.float32)
    for copy in range(12):
        for j in range(TAIL):
            tile[copy * TAIL + j, j] = 1
    join = np.zeros((6 * SX + 8, 8 * SX), np.float32)
    for la in range(SX):
        for k in range(7):
            join[6 * la + k, 8 * la + k] = 1
    return spread, spread.T.copy(), quad, tile, tile.T.copy(), join


def two(x):
    high = x.astype(BF16)
    return high, (x - high.astype(F32)).astype(BF16)


def dot(a, b):
    return jnp.dot(a, b, preferred_element_type=F32)


def dot_t(a, b):
    return lax.dot_general(a, b, (((1,), (1,)), ((), ())), preferred_element_type=F32)


def flag(condition):
    return jnp.where(condition, 1.0, 0.0).astype(BF16)


def basis(x):
    gaps = [x - r for r in LOBATTO_POINTS]
    before = [None] * 7
    after = [None] * 7
    for k in range(1, 7):
        before[k] = gaps[0] if k == 1 else before[k - 1] * gaps[k - 1]
    for k in range(5, -1, -1):
        after[k] = gaps[6] if k == 5 else after[k + 1] * gaps[k + 1]
    out = []
    for k in range(7):
        if k == 0:
            product = after[0]
        elif k == 6:
            product = before[6]
        else:
            product = before[k] * after[k]
        out.append(product * SCALE[k])
    return out


def head_mask(shape, part):
    lane = lax.broadcasted_iota(jnp.int32, shape, 1)
    return (lane >= HEAD * part) & (lane < HEAD * (part + 1))


def tail_mask(shape, part):
    lane = lax.broadcasted_iota(jnp.int32, shape, 2)
    row = lax.broadcasted_iota(jnp.int32, shape, 1)
    start = TAIL * (4 * part + row // 2)
    return (lane >= start) & (lane < start + TAIL)


def pack(rows, hot, tile, send, tiles, parts):
    first = rows[:HEAD]
    head = jnp.concatenate(
        [first, first, first, jnp.zeros((LANES - 3 * HEAD, first.shape[1]), F32)], axis=0
    )
    gathered = None
    for piece, tail in zip(two(head), two(rows[HEAD:])):
        both = jnp.concatenate([piece, dot(tile, tail).astype(BF16)], axis=0)
        term = dot_t(hot, both)
        gathered = term if gathered is None else gathered + term
    count = 8 * tiles
    for group in range(-(-parts // 3)):
        heads, tails = None, None
        for part in range(min(3, parts - 3 * group)):
            at = (3 * group + part) * count
            block = gathered[at : at + count, :LANES]
            block = jnp.where(head_mask(block.shape, part), block, 0.0)
            heads = block if heads is None else heads + block
            block = gathered[at : at + count, LANES:].reshape(tiles, 8, LANES)
            block = jnp.where(tail_mask(block.shape, part), block, 0.0)
            tails = block if tails is None else tails + block
        at = BLOCK * group
        send[:, at : at + 8, :] = heads.reshape(tiles, 8, LANES)
        send[:, at + 8 : at + 10, :] = (tails[:, 0:2] + tails[:, 2:4]) + (
            tails[:, 4:6] + tails[:, 6:8]
        )


def unpack(recv, fold, tiles, parts):
    count = 8 * tiles
    firsts, lasts = [], []
    for group in range(-(-parts // 3)):
        at = BLOCK * group
        turned = recv[:, at : at + 8, :].reshape(count, LANES).T
        pair = recv[:, at + 8 : at + 10, :]
        eight = jnp.concatenate([pair] * 4, axis=1)
        for part in range(min(3, parts - 3 * group)):
            firsts.append(turned[part * HEAD : (part + 1) * HEAD])
            lasts.append(
                jnp.where(tail_mask(eight.shape, part), eight, 0.0).reshape(count, LANES)
            )
    last = jnp.concatenate(lasts, axis=0)
    high, low = two(last)
    return jnp.concatenate(
        [jnp.concatenate(firsts, axis=1), dot_t(fold, high) + dot_t(fold, low)], axis=0
    )


def kernel(
    sizes,
    surf, coords, slaves, owners, lists, spread, spread_t, quad, tile_in, fold_in, join,
    out,
    held, lb1, lb2, value, tract, nodes, force_rows, elements, strips, pads,
    send1, recv1, send2, recv2, row_out, col_out, row_in, col_in, corner_in,
    ss1, rs1, ss2, rs2, hs, hr,
):
    wx, wy, parts, pairs, segs = sizes
    tiles = wx * wy
    body, gx, gy = lax.axis_index("body"), lax.axis_index("gx"), lax.axis_index("gy")
    other = 1 - body
    here = gx * wy + gy
    next_x, next_y = lax.rem(gx + 1, wx), lax.rem(gy + 1, wy)
    back_x, back_y = lax.rem(gx + wx - 1, wx), lax.rem(gy + wy - 1, wy)

    barrier = pltpu.get_barrier_semaphore()

    def greet(j, carry):
        to = lax.rem(here + j, tiles)
        pl.semaphore_signal(
            barrier, inc=1, device_id=(other, to // wy, lax.rem(to, wy)), device_id_type=MESH
        )
        return carry

    lax.fori_loop(0, tiles, greet, 0)
    for place in ((back_x, gy), (gx, back_y), (back_x, back_y)):
        pl.semaphore_signal(barrier, inc=1, device_id=(body,) + place, device_id_type=MESH)

    tile = tile_in[...].astype(BF16)
    fold = fold_in[...].astype(BF16)

    own = jnp.where(body == 0, lists[0], lists[1])
    pick = own.shape[1]
    column = jnp.broadcast_to(own, (LANES, pick)).T.reshape(tiles, parts, 8, LANES)
    column = jnp.concatenate(
        [column[:, part].reshape(8 * tiles, LANES) for part in range(parts)], axis=0
    )
    lane = lax.broadcasted_iota(jnp.int32, (pick, LANES), 1)
    list_hot = jnp.concatenate(
        [flag(column == lane + LANES * j) for j in range(segs // LANES)], axis=1
    )

    def copy_of(c, send, recv, ss, rs, to, land):
        return pltpu.make_async_remote_copy(
            src_ref=send.at[c, to],
            dst_ref=recv.at[c, land],
            send_sem=ss.at[c, to],
            recv_sem=rs.at[c, land],
            device_id=(other, to // wy, lax.rem(to, wy)),
            device_id_type=MESH,
        )

    def start_all(*where):
        def step(j, carry):
            copy_of(*where, lax.rem(here + j, tiles), here).start()
            return carry

        lax.fori_loop(0, tiles, step, 0)

    def wait_all(*where, arrive):
        def step(j, carry):
            copy = copy_of(*where, j, j)
            if arrive:
                copy.wait_recv()
            else:
                copy.wait_send()
            return carry

        lax.fori_loop(0, tiles, step, 0)

    there = (send1, recv1, ss1, rs1)
    back = (send2, recv2, ss2, rs2)

    held[...] = jnp.zeros_like(held)
    for c in range(3):
        held[c, :NODES, :] = surf[c * NODES : (c + 1) * NODES, 0, :]
        pack(held[c], list_hot, tile, send1.at[c], tiles, parts)
        if c == 0:
            pl.semaphore_wait(barrier, tiles + 3)
        start_all(c, *there)

    tile_row = lax.broadcasted_iota(jnp.int32, (tiles, pairs), 0)
    same = flag(tile_row == owners[...])
    earlier = flag(
        lax.broadcasted_iota(jnp.int32, (pairs, pairs), 0)
        < lax.broadcasted_iota(jnp.int32, (pairs, pairs), 1)
    )
    before = dot(same, earlier)
    rank = jnp.sum(before * same.astype(F32), axis=0, keepdims=True).astype(jnp.int32)
    part_of = rank // 8
    slot = part_of * (8 * tiles) + owners[...] * 8 + (rank - 8 * part_of)
    slot_hot = flag(lax.broadcasted_iota(jnp.int32, (8 * tiles * parts, pairs), 0) == slot)
    slave_hot = flag(lax.broadcasted_iota(jnp.int32, (segs, pairs), 0) == slaves[...])

    table_high, table_low = two(spread[...])
    back_high, back_low = two(spread_t[...])
    for c in range(3):
        high, low = two(held[c])
        high, low = two(dot(high, slave_hot) + dot(low, slave_hot))
        value[c] = dot(table_high, high) + (dot(table_high, low) + dot(table_low, high))

    for axis, store in ((0, lb1), (1, lb2)):
        place = jnp.concatenate(
            [coords[:, axis, :], jnp.zeros((QPAD - QUADS, pairs), F32)], axis=0
        )
        for chunk in range(QPAD // 8):
            at = slice(8 * chunk, 8 * chunk + 8)
            for k, factor in enumerate(basis(place[at])):
                store[k, at, :] = factor

    wide = SY * 6
    source = lax.broadcasted_iota(jnp.int32, (7 * SY, wide), 0)
    target = lax.broadcasted_iota(jnp.int32, (7 * SY, wide), 1)
    step_m = source // SY
    weave = flag(target == 6 * (source - step_m * SY) + step_m)
    together = join[...].astype(BF16)

    pads[...] = jnp.zeros_like(pads)
    force_rows[...] = jnp.zeros_like(force_rows)
    sign = 1.0 - 2.0 * body.astype(F32)
    blocks = [slice(b * LANES, (b + 1) * LANES) for b in range(pairs // LANES)]

    for c in range(3):
        wait_all(c, *there, arrive=True)
        high, low = two(unpack(recv1.at[c], fold, tiles, parts))
        nodes[...] = dot(high, slot_hot) + dot(low, slot_hot)
        for across in blocks:
            for chunk in range(QPAD // 8):
                at = slice(8 * chunk, 8 * chunk + 8)
                second = [lb2[k, at, across] for k in range(7)]
                total = None
                for k in range(7):
                    inner = None
                    for m in range(7):
                        row = 7 * k + m
                        term = second[m] * nodes[row : row + 1, across]
                        inner = term if inner is None else inner + term
                    term = lb1[k, at, across] * inner
                    total = term if total is None else total + term
                offset = total - value[c, at, across]
                if c < 2:
                    force = SHEAR * offset
                else:
                    gap = -sign * offset
                    soft = jnp.maximum(gap, 0.0) + jnp.log1p(jnp.exp(-jnp.abs(gap)))
                    force = -sign * KAPPA * soft
                tract[c, at, across] = force * quad[at, :]
        for across in blocks:
            minus = -tract[c, :, across]
            for m in range(7):
                weighted = lb2[m, :, across] * minus
                for k in range(7):
                    row = 7 * k + m
                    force_rows[row : row + 1, across] = jnp.sum(
                        lb1[k, :, across] * weighted, axis=0, keepdims=True
                    )
        pack(force_rows[...], slot_hot, tile, send2.at[c], tiles, parts)
        start_all(c, *back)

    for c in range(3):
        high, low = two(tract[c])
        slave_force = dot(back_high, high) + (dot(back_high, low) + dot(back_low, high))
        high, low = two(slave_force)
        elements[c] = dot_t(high, slave_hot) + dot_t(low, slave_hot)

    halos = []
    for c in range(3):
        wait_all(c, *back, arrive=True)
        high, low = two(unpack(recv2.at[c], fold, tiles, parts))
        total = elements[c] + (dot(high, list_hot) + dot(low, list_hot))
        for block in range(segs // LANES):
            strips[block] = total[:, block * LANES : (block + 1) * LANES]
        for m in range(7):
            for la in range(SX):
                block, lane = la * SY // LANES, la * SY % LANES
                rows = strips[block, pl.ds(m, 8, stride=7), :]
                pads[8 * la : 8 * la + 8, m * SY : (m + 1) * SY] = rows[:, lane : lane + SY]
        high, low = two(pads[...])
        joined = dot(together, high) + dot(together, low)
        col_out[c] = joined[:, 7 * SY - LANES :].T[LANES - 1 :, :]
        high, low = two(joined)
        grid = dot(high, weave) + dot(low, weave)
        out[c] = grid[: 6 * SX]
        row_out[c] = grid[6 * SX : 6 * SX + 1]
        messages = [
            (row_out.at[c], row_in.at[c], (next_x, gy)),
            (col_out.at[c], col_in.at[c], (gx, next_y)),
            (col_out.at[c], corner_in.at[c], (next_x, next_y)),
        ]
        for i, (src, dst, place) in enumerate(messages):
            copy = pltpu.make_async_remote_copy(
                src_ref=src,
                dst_ref=dst,
                send_sem=hs.at[c, i],
                recv_sem=hr.at[c, i],
                device_id=(body,) + place,
                device_id_type=MESH,
            )
            copy.start()
            halos.append(copy)

    for c in range(3):
        wait_all(c, *there, arrive=False)
        wait_all(c, *back, arrive=False)
    lanes = lax.broadcasted_iota(jnp.int32, (1, LANES), 1)
    for c in range(3):
        for copy in halos[3 * c : 3 * c + 3]:
            copy.wait_recv()
        corner = jnp.sum(
            jnp.where(lanes[:, : 6 * SX + 8] == 6 * SX, corner_in[c], 0.0), axis=1, keepdims=True
        )
        row = row_in[c]
        out[c, 0:1, :] = out[c, 0:1, :] + row
        edge = jnp.broadcast_to(col_in[c], (LANES, 6 * SX + 8)).T[: 6 * SX]
        first = (lax.broadcasted_iota(jnp.int32, edge.shape, 0) == 0).astype(F32)
        left = lax.broadcasted_iota(jnp.int32, edge.shape, 1) == 0
        out[c, :, :LANES] = out[c, :, :LANES] + jnp.where(left, edge + first * corner, 0.0)
    for copy in halos:
        copy.wait_send()


def local(surface_disp, proj_coords, pair_slave, pair_owner, send_list):
    wx, wy = lax.axis_size("gx"), lax.axis_size("gy")
    tiles = wx * wy
    segs = surface_disp.shape[-1]
    pairs = proj_coords.shape[-1]
    capacity = send_list.shape[-1] // tiles
    parts = -(-capacity // 8)
    slots = 8 * parts
    lists = send_list
    if slots != capacity:
        lists = lists.reshape(2, 1, tiles, capacity)
        lists = jnp.pad(lists, ((0, 0), (0, 0), (0, 0), (0, slots - capacity)), constant_values=-1)
        lists = lists.reshape(2, 1, tiles * slots)
    sizes = (wx, wy, parts, pairs, segs)
    vmem = pl.BlockSpec(memory_space=pltpu.VMEM)
    buffer = pltpu.VMEM((3, tiles, BLOCK * -(-parts // 3), LANES), F32)
    result = pl.pallas_call(
        functools.partial(kernel, sizes),
        out_shape=jax.ShapeDtypeStruct((3, 6 * SX, 6 * SY), F32),
        in_specs=[vmem] * 11,
        out_specs=vmem,
        scratch_shapes=[
            pltpu.VMEM((3, NPAD, segs), F32),
            pltpu.VMEM((7, QPAD, pairs), F32),
            pltpu.VMEM((7, QPAD, pairs), F32),
            pltpu.VMEM((3, QPAD, pairs), F32),
            pltpu.VMEM((3, QPAD, pairs), F32),
            pltpu.VMEM((NPAD, pairs), F32),
            pltpu.VMEM((NPAD, pairs), F32),
            pltpu.VMEM((3, NPAD, segs), F32),
            pltpu.VMEM((segs // LANES, NPAD, LANES), F32),
            pltpu.VMEM((8 * SX, 7 * SY), F32),
            buffer,
            buffer,
            buffer,
            buffer,
            pltpu.VMEM((3, 1, 6 * SY), F32),
            pltpu.VMEM((3, 1, 6 * SX + 8), F32),
            pltpu.VMEM((3, 1, 6 * SY), F32),
            pltpu.VMEM((3, 1, 6 * SX + 8), F32),
            pltpu.VMEM((3, 1, 6 * SX + 8), F32),
            pltpu.SemaphoreType.DMA((3, tiles)),
            pltpu.SemaphoreType.DMA((3, tiles)),
            pltpu.SemaphoreType.DMA((3, tiles)),
            pltpu.SemaphoreType.DMA((3, tiles)),
            pltpu.SemaphoreType.DMA((3, 3)),
            pltpu.SemaphoreType.DMA((3, 3)),
        ],
        compiler_params=pltpu.CompilerParams(
            collective_id=0, has_side_effects=True, vmem_limit_bytes=48 * 1024 * 1024
        ),
    )(
        surface_disp.reshape(3 * NODES, 1, segs),
        proj_coords[0].transpose(1, 0, 2),
        pair_slave,
        pair_owner.reshape(1, pairs),
        lists,
        *tables(),
    )
    return result[None]


def solution(mesh):
    return jax.shard_map(
        local,
        mesh=mesh,
        in_specs=(
            P("body", None, None, ("gx", "gy")),
            P("body", None, None, ("gx", "gy")),
            P("body", ("gx", "gy")),
            P("body", ("gx", "gy"), None),
            P(None, ("gx", "gy"), None),
        ),
        out_specs=P("body", None, "gx", "gy"),
        check_vma=False,
    )
```

```python
import functools

import jax
import jax.numpy as jnp
import numpy as np
from jax import lax
from jax.experimental import pallas as pl
from jax.experimental.pallas import tpu as pltpu
from jax.sharding import PartitionSpec as P

SX = 8
SY = 64
KAPPA = 2.0
SHEAR = 1.0
LOBATTO_POINTS = (
    -1.0,
    -0.830223896278567,
    -0.4688487934707142,
    0.0,
    0.4688487934707142,
    0.830223896278567,
    1.0,
)
GAUSS_POINTS = (
    -0.932469514203152,
    -0.6612093864662645,
    -0.2386191860831969,
    0.2386191860831969,
    0.6612093864662645,
    0.932469514203152,
)
GAUSS_WEIGHTS = (
    0.1713244923791704,
    0.3607615730481386,
    0.467913934572691,
    0.467913934572691,
    0.3607615730481386,
    0.1713244923791704,
)
MESH = pl.DeviceIdType.MESH
F32 = jnp.float32
BF16 = jnp.bfloat16
NODES = 49
NPAD = 56
LANES = 128
HEAD = 40
TAIL = NODES - HEAD
QUADS = 36
QPAD = 40
BLOCK = 10
SCALE = tuple(
    1.0 / float(np.prod([LOBATTO_POINTS[k] - LOBATTO_POINTS[m] for m in range(7) if m != k]))
    for k in range(7)
)


def tables():
    gauss = np.array(GAUSS_POINTS)
    single = np.ones((6, 7))
    for k in range(7):
        for m in range(7):
            if m != k:
                single[:, k] *= (gauss - LOBATTO_POINTS[m]) / (LOBATTO_POINTS[k] - LOBATTO_POINTS[m])
    spread = np.zeros((QPAD, NPAD), np.float32)
    spread[:QUADS, :NODES] = (single[:, None, :, None] * single[None, :, None, :]).reshape(
        QUADS, NODES
    )
    weights = np.array(GAUSS_WEIGHTS)
    quad = np.zeros((QPAD, LANES), np.float32)
    quad[:QUADS] = (weights[:, None] * weights[None, :]).reshape(QUADS, 1)
    table = np.zeros((QPAD + NPAD + QPAD, LANES), np.float32)
    table[:QPAD, :NPAD] = spread
    table[QPAD : QPAD + NPAD, :QPAD] = spread.T
    table[QPAD + NPAD :] = quad
    return table


def two(x):
    high = x.astype(BF16)
    return high, (x - high.astype(F32)).astype(BF16)


def dot(a, b):
    return jnp.dot(a, b, preferred_element_type=F32)


def dot_t(a, b):
    return lax.dot_general(a, b, (((1,), (1,)), ((), ())), preferred_element_type=F32)


def flag(condition):
    return jnp.where(condition, 1.0, 0.0).astype(BF16)


def basis(x):
    gaps = [x - r for r in LOBATTO_POINTS]
    before = [None] * 7
    after = [None] * 7
    for k in range(1, 7):
        before[k] = gaps[0] if k == 1 else before[k - 1] * gaps[k - 1]
    for k in range(5, -1, -1):
        after[k] = gaps[6] if k == 5 else after[k + 1] * gaps[k + 1]
    out = []
    for k in range(7):
        if k == 0:
            product = after[0]
        elif k == 6:
            product = before[6]
        else:
            product = before[k] * after[k]
        out.append(product * SCALE[k])
    return out


def iota(shape, axis):
    return lax.broadcasted_iota(jnp.int32, shape, axis)


def head_mask(part):
    lane = iota((1, LANES), 1)
    return jnp.where((lane >= HEAD * part) & (lane < HEAD * (part + 1)), 1.0, 0.0)


def tail_mask(part):
    lane = iota((1, 8, LANES), 2)
    start = TAIL * (4 * part + iota((1, 8, LANES), 1) // 2)
    return jnp.where((lane >= start) & (lane < start + TAIL), 1.0, 0.0)


def pack(rows, hot, tile, send, tiles, parts):
    first = rows[:HEAD]
    head = jnp.concatenate(
        [first, first, first, jnp.zeros((LANES - 3 * HEAD, first.shape[1]), F32)], axis=0
    )
    gathered = None
    for piece, tail in zip(two(head), two(rows[HEAD:])):
        both = jnp.concatenate([piece, dot(tile, tail).astype(BF16)], axis=0)
        term = dot_t(hot, both)
        gathered = term if gathered is None else gathered + term
    count = 8 * tiles
    for group in range(-(-parts // 3)):
        heads, tails = None, None
        for part in range(min(3, parts - 3 * group)):
            at = (3 * group + part) * count
            block = gathered[at : at + count, :LANES]
            block = block * head_mask(part)
            heads = block if heads is None else heads + block
            block = gathered[at : at + count, LANES:].reshape(tiles, 8, LANES)
            block = block * tail_mask(part)
            tails = block if tails is None else tails + block
        at = BLOCK * group
        send[:, at : at + 8, :] = heads.reshape(tiles, 8, LANES)
        send[:, at + 8 : at + 10, :] = (tails[:, 0:2] + tails[:, 2:4]) + (
            tails[:, 4:6] + tails[:, 6:8]
        )


def unpack(recv, fold, tiles, parts):
    count = 8 * tiles
    firsts, lasts = [], []
    for group in range(-(-parts // 3)):
        at = BLOCK * group
        turned = recv[:, at : at + 8, :].reshape(count, LANES).T
        pair = recv[:, at + 8 : at + 10, :]
        eight = jnp.concatenate([pair] * 4, axis=1)
        for part in range(min(3, parts - 3 * group)):
            firsts.append(turned[part * HEAD : (part + 1) * HEAD])
            lasts.append((eight * tail_mask(part)).reshape(count, LANES))
    last = jnp.concatenate(lasts, axis=0)
    high, low = two(last)
    return jnp.concatenate(
        [jnp.concatenate(firsts, axis=1), dot_t(fold, high) + dot_t(fold, low)], axis=0
    )


def kernel(
    sizes,
    surf_in, coords_in, slaves_in, owners_in, lists_in, table_in,
    out,
    surf, coords, slaves, owners, lists, table,
    held, lb1, lb2, value, tract, nodes, force_rows, elements, strips, pads,
    send1, recv1, send2, recv2, row_out, col_out, row_in, col_in, corner_in,
    ss1, rs1, ss2, rs2, hs, hr, loads,
):
    wx, wy, parts, pairs, segs = sizes
    tiles = wx * wy
    body, gx, gy = lax.axis_index("body"), lax.axis_index("gx"), lax.axis_index("gy")
    other = 1 - body
    here = gx * wy + gy
    next_x, next_y = lax.rem(gx + 1, wx), lax.rem(gy + 1, wy)
    back_x, back_y = lax.rem(gx + wx - 1, wx), lax.rem(gy + wy - 1, wy)

    operands = (
        (lists_in, lists), (surf_in, surf), (owners_in, owners),
        (slaves_in, slaves), (table_in, table), (coords_in, coords),
    )
    reads = [
        pltpu.make_async_copy(src, dst, loads.at[i]) for i, (src, dst) in enumerate(operands)
    ]
    for read in reads:
        read.start()

    def repeat(step):
        if tiles <= 16:
            for j in range(tiles):
                step(j)
        else:
            lax.fori_loop(0, tiles, lambda j, carry: (step(j), carry)[1], 0)

    barrier = pltpu.get_barrier_semaphore()

    def greet(j):
        to = lax.rem(here + j, tiles)
        pl.semaphore_signal(
            barrier, inc=1, device_id=(other, to // wy, lax.rem(to, wy)), device_id_type=MESH
        )

    repeat(greet)
    for place in ((back_x, gy), (gx, back_y), (back_x, back_y)):
        pl.semaphore_signal(barrier, inc=1, device_id=(body,) + place, device_id_type=MESH)

    row, step = iota((LANES, 16), 0), iota((LANES, 16), 1)
    tile = flag((row - TAIL * (row // TAIL) == step) & (row < 12 * TAIL))
    row, step = iota((16, LANES), 1), iota((16, LANES), 0)
    fold = flag((row - TAIL * (row // TAIL) == step) & (row < 12 * TAIL))
    row, step = iota((6 * SX + 8, 8 * SX), 0), iota((6 * SX + 8, 8 * SX), 1)
    la = step // 8
    together = flag((row == 6 * la + (step - 8 * la)) & (step - 8 * la < 7))
    reads[0].wait()

    own = jnp.where(body == 0, lists[0], lists[1])
    pick = own.shape[1]
    column = jnp.broadcast_to(own, (LANES, pick)).T.reshape(tiles, parts, 8, LANES)
    column = jnp.concatenate(
        [column[:, part].reshape(8 * tiles, LANES) for part in range(parts)], axis=0
    )
    lane = lax.broadcasted_iota(jnp.int32, (pick, LANES), 1)
    list_hot = jnp.concatenate(
        [flag(column == lane + LANES * j) for j in range(segs // LANES)], axis=1
    )

    def copy_of(c, send, recv, ss, rs, to, land):
        return pltpu.make_async_remote_copy(
            src_ref=send.at[c, to],
            dst_ref=recv.at[c, land],
            send_sem=ss.at[c],
            recv_sem=rs.at[c],
            device_id=(other, to // wy, lax.rem(to, wy)),
            device_id_type=MESH,
        )

    def start_all(*where):
        repeat(lambda j: copy_of(*where, lax.rem(here + j, tiles), here).start())

    def wait_all(c, send, recv, ss, rs, arrive):
        whole, sem = (recv, rs) if arrive else (send, ss)
        pltpu.make_async_copy(whole.at[c], whole.at[c], sem.at[c]).wait()

    there = (send1, recv1, ss1, rs1)
    back = (send2, recv2, ss2, rs2)

    held[...] = jnp.zeros_like(held)
    reads[1].wait()
    for c in range(3):
        held[c, :NODES, :] = surf[c * NODES : (c + 1) * NODES, 0, :]
        pack(held[c], list_hot, tile, send1.at[c], tiles, parts)
        if c == 0:
            pl.semaphore_wait(barrier, tiles + 3)
        start_all(c, *there)

    for read in reads[2:]:
        read.wait()
    tile_row = lax.broadcasted_iota(jnp.int32, (tiles, pairs), 0)
    same = flag(tile_row == owners[...])
    earlier = flag(
        lax.broadcasted_iota(jnp.int32, (pairs, pairs), 0)
        < lax.broadcasted_iota(jnp.int32, (pairs, pairs), 1)
    )
    before = dot(same, earlier)
    rank = jnp.sum(before * same.astype(F32), axis=0, keepdims=True).astype(jnp.int32)
    part_of = rank // 8
    slot = part_of * (8 * tiles) + owners[...] * 8 + (rank - 8 * part_of)
    slot_hot = flag(lax.broadcasted_iota(jnp.int32, (8 * tiles * parts, pairs), 0) == slot)
    slave_hot = flag(lax.broadcasted_iota(jnp.int32, (segs, pairs), 0) == slaves[...])

    table_high, table_low = two(table[:QPAD, :NPAD])
    back_high, back_low = two(table[QPAD : QPAD + NPAD, :QPAD])
    for c in range(3):
        high, low = two(held[c])
        high, low = two(dot(high, slave_hot) + dot(low, slave_hot))
        value[c] = dot(table_high, high) + (dot(table_high, low) + dot(table_low, high))

    for axis, store in ((0, lb1), (1, lb2)):
        place = jnp.concatenate(
            [coords[:, axis, :], jnp.zeros((QPAD - QUADS, pairs), F32)], axis=0
        )
        for chunk in range(QPAD // 8):
            at = slice(8 * chunk, 8 * chunk + 8)
            for k, factor in enumerate(basis(place[at])):
                store[k, at, :] = factor

    wide = SY * 6
    source = lax.broadcasted_iota(jnp.int32, (7 * SY, wide), 0)
    target = lax.broadcasted_iota(jnp.int32, (7 * SY, wide), 1)
    step_m = source // SY
    weave = flag(target == 6 * (source - step_m * SY) + step_m)

    pads[...] = jnp.zeros_like(pads)
    force_rows[...] = jnp.zeros_like(force_rows)
    sign = 1.0 - 2.0 * body.astype(F32)
    blocks = [slice(b * LANES, (b + 1) * LANES) for b in range(pairs // LANES)]

    for c in range(3):
        wait_all(c, *there, arrive=True)
        high, low = two(unpack(recv1.at[c], fold, tiles, parts))
        nodes[...] = dot(high, slot_hot) + dot(low, slot_hot)
        for across in blocks:
            for chunk in range(QPAD // 8):
                at = slice(8 * chunk, 8 * chunk + 8)
                second = [lb2[k, at, across] for k in range(7)]
                total = None
                for k in range(7):
                    inner = None
                    for m in range(7):
                        row = 7 * k + m
                        term = second[m] * nodes[row : row + 1, across]
                        inner = term if inner is None else inner + term
                    term = lb1[k, at, across] * inner
                    total = term if total is None else total + term
                offset = total - value[c, at, across]
                if c < 2:
                    force = SHEAR * offset
                else:
                    gap = -sign * offset
                    soft = jnp.maximum(gap, 0.0) + jnp.log1p(jnp.exp(-jnp.abs(gap)))
                    force = -sign * KAPPA * soft
                tract[c, at, across] = force * table[QPAD + NPAD + 8 * chunk : QPAD + NPAD + 8 * chunk + 8, :]
        for across in blocks:
            minus = -tract[c, :, across]
            for m in range(7):
                weighted = lb2[m, :, across] * minus
                for k in range(7):
                    row = 7 * k + m
                    force_rows[row : row + 1, across] = jnp.sum(
                        lb1[k, :, across] * weighted, axis=0, keepdims=True
                    )
        pack(force_rows[...], slot_hot, tile, send2.at[c], tiles, parts)
        start_all(c, *back)

    for c in range(3):
        high, low = two(tract[c])
        slave_force = dot(back_high, high) + (dot(back_high, low) + dot(back_low, high))
        high, low = two(slave_force)
        elements[c] = dot_t(high, slave_hot) + dot_t(low, slave_hot)

    halos = []
    for c in range(3):
        wait_all(c, *back, arrive=True)
        high, low = two(unpack(recv2.at[c], fold, tiles, parts))
        total = elements[c] + (dot(high, list_hot) + dot(low, list_hot))
        for block in range(segs // LANES):
            strips[block] = total[:, block * LANES : (block + 1) * LANES]
        for m in range(7):
            for la in range(SX):
                block, lane = la * SY // LANES, la * SY % LANES
                rows = strips[block, pl.ds(m, 8, stride=7), :]
                pads[8 * la : 8 * la + 8, m * SY : (m + 1) * SY] = rows[:, lane : lane + SY]
        high, low = two(pads[...])
        joined = dot(together, high) + dot(together, low)
        col_out[c] = joined[:, 7 * SY - LANES :].T[LANES - 1 :, :]
        high, low = two(joined)
        grid = dot(high, weave) + dot(low, weave)
        out[c] = grid[: 6 * SX]
        row_out[c] = grid[6 * SX : 6 * SX + 1]
        messages = [
            (row_out.at[c], row_in.at[c], (next_x, gy)),
            (col_out.at[c], col_in.at[c], (gx, next_y)),
            (col_out.at[c], corner_in.at[c], (next_x, next_y)),
        ]
        for i, (src, dst, place) in enumerate(messages):
            copy = pltpu.make_async_remote_copy(
                src_ref=src,
                dst_ref=dst,
                send_sem=hs.at[c, i],
                recv_sem=hr.at[c, i],
                device_id=(body,) + place,
                device_id_type=MESH,
            )
            copy.start()
            halos.append(copy)

    for c in range(3):
        wait_all(c, *there, arrive=False)
        wait_all(c, *back, arrive=False)
    lanes = lax.broadcasted_iota(jnp.int32, (1, LANES), 1)
    for c in range(3):
        for copy in halos[3 * c : 3 * c + 3]:
            copy.wait_recv()
        corner = jnp.sum(
            jnp.where(lanes[:, : 6 * SX + 8] == 6 * SX, corner_in[c], 0.0), axis=1, keepdims=True
        )
        row = row_in[c]
        out[c, 0:1, :] = out[c, 0:1, :] + row
        edge = jnp.broadcast_to(col_in[c], (LANES, 6 * SX + 8)).T[: 6 * SX]
        first = (lax.broadcasted_iota(jnp.int32, edge.shape, 0) == 0).astype(F32)
        left = lax.broadcasted_iota(jnp.int32, edge.shape, 1) == 0
        out[c, :, :LANES] = out[c, :, :LANES] + jnp.where(left, edge + first * corner, 0.0)
    for copy in halos:
        copy.wait_send()


def local(surface_disp, proj_coords, pair_slave, pair_owner, send_list):
    wx, wy = lax.axis_size("gx"), lax.axis_size("gy")
    tiles = wx * wy
    segs = surface_disp.shape[-1]
    pairs = proj_coords.shape[-1]
    capacity = send_list.shape[-1] // tiles
    parts = -(-capacity // 8)
    slots = 8 * parts
    lists = send_list
    if slots != capacity:
        lists = lists.reshape(2, 1, tiles, capacity)
        lists = jnp.pad(lists, ((0, 0), (0, 0), (0, 0), (0, slots - capacity)), constant_values=-1)
        lists = lists.reshape(2, 1, tiles * slots)
    sizes = (wx, wy, parts, pairs, segs)
    vmem = pl.BlockSpec(memory_space=pltpu.VMEM)
    buffer = pltpu.VMEM((3, tiles, BLOCK * -(-parts // 3), LANES), F32)
    result = pl.pallas_call(
        functools.partial(kernel, sizes),
        out_shape=jax.ShapeDtypeStruct((3, 6 * SX, 6 * SY), F32),
        in_specs=[pl.BlockSpec(memory_space=pl.ANY)] * 6,
        out_specs=vmem,
        scratch_shapes=[
            pltpu.VMEM((3 * NODES, 1, segs), F32),
            pltpu.VMEM((QUADS, 2, pairs), F32),
            pltpu.VMEM((1, pairs), jnp.int32),
            pltpu.VMEM((1, pairs), jnp.int32),
            pltpu.VMEM((2, 1, tiles * slots), jnp.int32),
            pltpu.VMEM((QPAD + NPAD + QPAD, LANES), F32),
            pltpu.VMEM((3, NPAD, segs), F32),
            pltpu.VMEM((7, QPAD, pairs), F32),
            pltpu.VMEM((7, QPAD, pairs), F32),
            pltpu.VMEM((3, QPAD, pairs), F32),
            pltpu.VMEM((3, QPAD, pairs), F32),
            pltpu.VMEM((NPAD, pairs), F32),
            pltpu.VMEM((NPAD, pairs), F32),
            pltpu.VMEM((3, NPAD, segs), F32),
            pltpu.VMEM((segs // LANES, NPAD, LANES), F32),
            pltpu.VMEM((8 * SX, 7 * SY), F32),
            buffer,
            buffer,
            buffer,
            buffer,
            pltpu.VMEM((3, 1, 6 * SY), F32),
            pltpu.VMEM((3, 1, 6 * SX + 8), F32),
            pltpu.VMEM((3, 1, 6 * SY), F32),
            pltpu.VMEM((3, 1, 6 * SX + 8), F32),
            pltpu.VMEM((3, 1, 6 * SX + 8), F32),
            pltpu.SemaphoreType.DMA((3,)),
            pltpu.SemaphoreType.DMA((3,)),
            pltpu.SemaphoreType.DMA((3,)),
            pltpu.SemaphoreType.DMA((3,)),
            pltpu.SemaphoreType.DMA((3, 3)),
            pltpu.SemaphoreType.DMA((3, 3)),
            pltpu.SemaphoreType.DMA((6,)),
        ],
        compiler_params=pltpu.CompilerParams(
            collective_id=0, has_side_effects=True, vmem_limit_bytes=60 * 1024 * 1024
        ),
    )(
        surface_disp.reshape(3 * NODES, 1, segs),
        proj_coords[0].transpose(1, 0, 2),
        pair_slave,
        pair_owner.reshape(1, pairs),
        lists,
        tables(),
    )
    return result[None]


def solution(mesh):
    return jax.shard_map(
        local,
        mesh=mesh,
        in_specs=(
            P("body", None, None, ("gx", "gy")),
            P("body", None, None, ("gx", "gy")),
            P("body", ("gx", "gy")),
            P("body", ("gx", "gy"), None),
            P(None, ("gx", "gy"), None),
        ),
        out_specs=P("body", None, "gx", "gy"),
        check_vma=False,
    )
```

```python
import functools

import jax
import jax.numpy as jnp
import numpy as np
from jax import lax
from jax.experimental import pallas as pl
from jax.experimental.pallas import tpu as pltpu
from jax.sharding import PartitionSpec as P

SX = 8
SY = 64
KAPPA = 2.0
SHEAR = 1.0
LOBATTO_POINTS = (
    -1.0,
    -0.830223896278567,
    -0.4688487934707142,
    0.0,
    0.4688487934707142,
    0.830223896278567,
    1.0,
)
GAUSS_POINTS = (
    -0.932469514203152,
    -0.6612093864662645,
    -0.2386191860831969,
    0.2386191860831969,
    0.6612093864662645,
    0.932469514203152,
)
GAUSS_WEIGHTS = (
    0.1713244923791704,
    0.3607615730481386,
    0.467913934572691,
    0.467913934572691,
    0.3607615730481386,
    0.1713244923791704,
)
MESH = pl.DeviceIdType.MESH
F32 = jnp.float32
BF16 = jnp.bfloat16
NODES = 49
NPAD = 64
LANES = 128
HEAD = 40
TAIL = NODES - HEAD
QUADS = 36
QPAD = 40
QROWS = 48
XPAD = 64
BLOCK = 10
SCALE = tuple(
    1.0 / float(np.prod([LOBATTO_POINTS[k] - LOBATTO_POINTS[m] for m in range(7) if m != k]))
    for k in range(7)
)


def tables():
    gauss = np.array(GAUSS_POINTS)
    single = np.ones((6, 7))
    for k in range(7):
        for m in range(7):
            if m != k:
                single[:, k] *= (gauss - LOBATTO_POINTS[m]) / (LOBATTO_POINTS[k] - LOBATTO_POINTS[m])
    spread = np.zeros((QPAD, NPAD), np.float32)
    spread[:QUADS, :NODES] = (single[:, None, :, None] * single[None, :, None, :]).reshape(
        QUADS, NODES
    )
    weights = np.array(GAUSS_WEIGHTS)
    quad = np.zeros((QPAD, LANES), np.float32)
    quad[:QUADS] = (weights[:, None] * weights[None, :]).reshape(QUADS, 1)
    high = spread.astype(BF16).astype(np.float32)
    low = (spread - high).astype(BF16).astype(np.float32)
    table = np.zeros((QPAD + NPAD + QPAD, 2 * LANES), np.float32)
    for i, part in enumerate((high, high, low)):
        table[:QPAD, i * NPAD : (i + 1) * NPAD] = part
        table[QPAD : QPAD + NPAD, i * QROWS : i * QROWS + QPAD] = part.T
    table[QPAD + NPAD :, :LANES] = quad
    return table


def two(x):
    high = x.astype(BF16)
    return high, (x - high.astype(F32)).astype(BF16)


def dot(a, b):
    return jnp.dot(a, b, preferred_element_type=F32)


def dot_t(a, b):
    return lax.dot_general(a, b, (((1,), (1,)), ((), ())), preferred_element_type=F32)


def dot_parts(x, b):
    rows = x.shape[0]
    both = dot(jnp.concatenate(two(x), axis=0), b)
    return both[:rows] + both[rows:]


def dot_parts_t(x, b):
    rows = x.shape[0]
    both = dot_t(jnp.concatenate(two(x), axis=0), b)
    return both[:rows] + both[rows:]


def flag(condition):
    return jnp.where(condition, 1.0, 0.0).astype(BF16)


def basis(x):
    gaps = [x - r for r in LOBATTO_POINTS]
    before = [None] * 7
    after = [None] * 7
    for k in range(1, 7):
        before[k] = gaps[0] if k == 1 else before[k - 1] * gaps[k - 1]
    for k in range(5, -1, -1):
        after[k] = gaps[6] if k == 5 else after[k + 1] * gaps[k + 1]
    out = []
    for k in range(7):
        if k == 0:
            product = after[0]
        elif k == 6:
            product = before[6]
        else:
            product = before[k] * after[k]
        out.append(product * SCALE[k])
    return out


def iota(shape, axis):
    return lax.broadcasted_iota(jnp.int32, shape, axis)


def head_mask(part):
    lane = iota((1, LANES), 1)
    return jnp.where((lane >= HEAD * part) & (lane < HEAD * (part + 1)), 1.0, 0.0)


def tail_mask(part):
    lane = iota((1, 8, LANES), 2)
    start = TAIL * (4 * part + iota((1, 8, LANES), 1) // 2)
    return jnp.where((lane >= start) & (lane < start + TAIL), 1.0, 0.0)


def pack(rows, hot, tile, send, tiles, parts):
    first = rows[:HEAD]
    head = jnp.concatenate(
        [first, first, first, jnp.zeros((LANES - 3 * HEAD, first.shape[1]), F32)], axis=0
    )
    tails = jnp.concatenate(two(rows[HEAD : HEAD + 16]), axis=0)
    tails = dot(tile, tails).astype(BF16)
    high, low = two(head)
    gathered = dot_t(hot, jnp.concatenate([high, tails[:LANES]], axis=0)) + dot_t(
        hot, jnp.concatenate([low, tails[LANES:]], axis=0)
    )
    count = 8 * tiles
    for group in range(-(-parts // 3)):
        heads, tails = None, None
        for part in range(min(3, parts - 3 * group)):
            at = (3 * group + part) * count
            block = gathered[at : at + count, :LANES]
            block = block * head_mask(part)
            heads = block if heads is None else heads + block
            block = gathered[at : at + count, LANES:].reshape(tiles, 8, LANES)
            block = block * tail_mask(part)
            tails = block if tails is None else tails + block
        at = BLOCK * group
        send[:, at : at + 8, :] = heads.reshape(tiles, 8, LANES)
        send[:, at + 8 : at + 10, :] = (tails[:, 0:2] + tails[:, 2:4]) + (
            tails[:, 4:6] + tails[:, 6:8]
        )


def unpack(recv, fold, tiles, parts):
    count = 8 * tiles
    firsts, lasts = [], []
    for group in range(-(-parts // 3)):
        at = BLOCK * group
        turned = recv[:, at : at + 8, :].reshape(count, LANES).T
        pair = recv[:, at + 8 : at + 10, :]
        eight = jnp.concatenate([pair] * 4, axis=1)
        for part in range(min(3, parts - 3 * group)):
            firsts.append(turned[part * HEAD : (part + 1) * HEAD])
            lasts.append((eight * tail_mask(part)).reshape(count, LANES))
    last = jnp.concatenate(lasts, axis=0)
    return jnp.concatenate(
        [jnp.concatenate(firsts, axis=1), dot_t(fold, jnp.concatenate(two(last), axis=1))], axis=0
    )


def kernel(
    sizes,
    surf_in, coords_in, slaves_in, owners_in, lists_in, table_in,
    out,
    surf, coords, slaves, owners, lists, table,
    held, lb1, lb2, value, tract, nodes, force_rows, elements, strips, pads,
    send1, recv1, send2, recv2, row_out, col_out, row_in, col_in, corner_in,
    ss1, rs1, ss2, rs2, hs, hr, loads,
):
    wx, wy, parts, pairs, segs = sizes
    tiles = wx * wy
    body, gx, gy = lax.axis_index("body"), lax.axis_index("gx"), lax.axis_index("gy")
    other = 1 - body
    here = gx * wy + gy
    next_x, next_y = lax.rem(gx + 1, wx), lax.rem(gy + 1, wy)
    back_x, back_y = lax.rem(gx + wx - 1, wx), lax.rem(gy + wy - 1, wy)

    operands = (
        (lists_in, lists), (surf_in, surf), (owners_in, owners),
        (slaves_in, slaves), (table_in, table), (coords_in, coords),
    )
    reads = [
        pltpu.make_async_copy(src, dst, loads.at[i]) for i, (src, dst) in enumerate(operands)
    ]
    for read in reads:
        read.start()

    def repeat(step):
        if tiles <= 16:
            for j in range(tiles):
                step(j)
        else:
            lax.fori_loop(0, tiles, lambda j, carry: (step(j), carry)[1], 0)

    barrier = pltpu.get_barrier_semaphore()

    def greet(j):
        to = lax.rem(here + j, tiles)
        pl.semaphore_signal(
            barrier, inc=1, device_id=(other, to // wy, lax.rem(to, wy)), device_id_type=MESH
        )

    repeat(greet)
    for place in ((back_x, gy), (gx, back_y), (back_x, back_y)):
        pl.semaphore_signal(barrier, inc=1, device_id=(body,) + place, device_id_type=MESH)

    row, step = iota((2 * LANES, 32), 0), iota((2 * LANES, 32), 1)
    place = row - LANES * (row // LANES)
    copy = place // TAIL
    tile = flag((place - TAIL * copy + 16 * (row // LANES) == step) & (copy < 12))
    row, step = iota((24, 2 * LANES), 1), iota((24, 2 * LANES), 0)
    place = row - LANES * (row // LANES)
    copy = place // TAIL
    fold = flag((place - TAIL * copy == step) & (copy < 12))
    row, step = iota((XPAD, 16 * SX), 0), iota((XPAD, 16 * SX), 1)
    step = step - 8 * SX * (step // (8 * SX))
    la = step // 8
    together = flag((row == 6 * la + (step - 8 * la)) & (step - 8 * la < 7))
    reads[0].wait()

    own = jnp.where(body == 0, lists[0], lists[1])
    pick = own.shape[1]
    column = jnp.broadcast_to(own, (LANES, pick)).T.reshape(tiles, parts, 8, LANES)
    column = jnp.concatenate(
        [column[:, part].reshape(8 * tiles, LANES) for part in range(parts)], axis=0
    )
    lane = lax.broadcasted_iota(jnp.int32, (pick, LANES), 1)
    list_hot = jnp.concatenate(
        [flag(column == lane + LANES * j) for j in range(segs // LANES)], axis=1
    )

    def copy_of(c, send, recv, ss, rs, to, land):
        return pltpu.make_async_remote_copy(
            src_ref=send.at[c, to],
            dst_ref=recv.at[c, land],
            send_sem=ss.at[c],
            recv_sem=rs.at[c],
            device_id=(other, to // wy, lax.rem(to, wy)),
            device_id_type=MESH,
        )

    def start_all(*where):
        half = wy // 2 + tiles
        repeat(lambda j: copy_of(*where, lax.rem(here + half - j, tiles), here).start())

    def wait_all(c, send, recv, ss, rs, arrive):
        whole, sem = (recv, rs) if arrive else (send, ss)
        pltpu.make_async_copy(whole.at[c], whole.at[c], sem.at[c]).wait()

    there = (send1, recv1, ss1, rs1)
    back = (send2, recv2, ss2, rs2)

    held[...] = jnp.zeros_like(held)
    reads[1].wait()
    for c in range(3):
        held[c, :NODES, :] = surf[c * NODES : (c + 1) * NODES, 0, :]
        pack(held[c], list_hot, tile, send1.at[c], tiles, parts)
        if c == 0:
            pl.semaphore_wait(barrier, tiles + 3)
        start_all(c, *there)

    for read in reads[2:]:
        read.wait()
    tile_row = lax.broadcasted_iota(jnp.int32, (tiles, pairs), 0)
    same = flag(tile_row == owners[...])
    earlier = flag(
        lax.broadcasted_iota(jnp.int32, (pairs, pairs), 0)
        < lax.broadcasted_iota(jnp.int32, (pairs, pairs), 1)
    )
    before = dot(same, earlier)
    rank = jnp.sum(before * same.astype(F32), axis=0, keepdims=True).astype(jnp.int32)
    part_of = rank // 8
    slot = part_of * (8 * tiles) + owners[...] * 8 + (rank - 8 * part_of)
    slot_hot = flag(lax.broadcasted_iota(jnp.int32, (8 * tiles * parts, pairs), 0) == slot)
    slave_hot = flag(lax.broadcasted_iota(jnp.int32, (segs, pairs), 0) == slaves[...])

    spread = table[:QPAD, : 3 * NPAD].astype(BF16)
    for c in range(3):
        high, low = two(dot_parts(held[c], slave_hot))
        value[c] = dot(spread, jnp.concatenate([high, low, high], axis=0))

    for axis, store in ((0, lb1), (1, lb2)):
        place = jnp.concatenate(
            [coords[:, axis, :], jnp.zeros((QPAD - QUADS, pairs), F32)], axis=0
        )
        for chunk in range(QPAD // 8):
            at = slice(8 * chunk, 8 * chunk + 8)
            for k, factor in enumerate(basis(place[at])):
                store[k, at, :] = factor

    pads[...] = jnp.zeros_like(pads)
    force_rows[...] = jnp.zeros_like(force_rows)
    sign = 1.0 - 2.0 * body.astype(F32)
    blocks = [slice(b * LANES, (b + 1) * LANES) for b in range(pairs // LANES)]

    for c in range(3):
        wait_all(c, *there, arrive=True)
        nodes[...] = dot_parts(unpack(recv1.at[c], fold, tiles, parts), slot_hot)
        for across in blocks:
            for chunk in range(QPAD // 8):
                at = slice(8 * chunk, 8 * chunk + 8)
                second = [lb2[k, at, across] for k in range(7)]
                weight = table[QPAD + NPAD + 8 * chunk : QPAD + NPAD + 8 * chunk + 8, :LANES]
                total = None
                for k in range(7):
                    inner = None
                    for m in range(7):
                        row = 7 * k + m
                        term = second[m] * nodes[row : row + 1, across]
                        inner = term if inner is None else inner + term
                    term = lb1[k, at, across] * inner
                    total = term if total is None else total + term
                offset = total - value[c, at, across]
                if c < 2:
                    force = SHEAR * offset
                else:
                    gap = -sign * offset
                    soft = jnp.maximum(gap, 0.0) + jnp.log1p(jnp.exp(-jnp.abs(gap)))
                    force = -sign * KAPPA * soft
                tract[c, at, across] = force * weight
        for across in blocks:
            minus = -tract[c, :, across]
            for m in range(7):
                weighted = lb2[m, :, across] * minus
                for k in range(7):
                    row = 7 * k + m
                    force_rows[row : row + 1, across] = jnp.sum(
                        lb1[k, :, across] * weighted, axis=0, keepdims=True
                    )
        pack(force_rows[...], slot_hot, tile, send2.at[c], tiles, parts)
        start_all(c, *back)

    spread_t = table[QPAD : QPAD + NPAD, : 3 * QROWS].astype(BF16)
    empty = jnp.zeros((QROWS - QPAD, pairs), F32)
    for c in range(3):
        high, low = two(jnp.concatenate([tract[c], empty], axis=0))
        slave_force = dot(spread_t, jnp.concatenate([high, low, high], axis=0))
        elements[c] = dot_parts_t(slave_force, slave_hot)

    wide = SY * 6
    source = lax.broadcasted_iota(jnp.int32, (7 * SY, wide), 0)
    target = lax.broadcasted_iota(jnp.int32, (7 * SY, wide), 1)
    step_m = source // SY
    weave = flag(target == 6 * (source - step_m * SY) + step_m)

    halos = []
    for c in range(3):
        wait_all(c, *back, arrive=True)
        total = elements[c] + dot_parts(unpack(recv2.at[c], fold, tiles, parts), list_hot)
        for block in range(segs // LANES):
            strips[block] = total[:, block * LANES : (block + 1) * LANES]
        for m in range(7):
            for la in range(SX):
                block, lane = la * SY // LANES, la * SY % LANES
                rows = strips[block, pl.ds(m, 8, stride=7), :]
                pads[8 * la : 8 * la + 8, m * SY : (m + 1) * SY] = rows[:, lane : lane + SY]
        joined = dot(together, jnp.concatenate(two(pads[...]), axis=0))
        col_out[c] = joined[:, 7 * SY - LANES :].T[LANES - 1 :, :]
        grid = dot_parts(joined, weave)
        out[c] = grid[: 6 * SX]
        row_out[c] = grid[6 * SX : 6 * SX + 1]
        messages = [
            (row_out.at[c], row_in.at[c], (next_x, gy)),
            (col_out.at[c], col_in.at[c], (gx, next_y)),
            (col_out.at[c], corner_in.at[c], (next_x, next_y)),
        ]
        for i, (src, dst, place) in enumerate(messages):
            copy = pltpu.make_async_remote_copy(
                src_ref=src,
                dst_ref=dst,
                send_sem=hs.at[c, i],
                recv_sem=hr.at[c, i],
                device_id=(body,) + place,
                device_id_type=MESH,
            )
            copy.start()
            halos.append(copy)

    for c in range(3):
        wait_all(c, *there, arrive=False)
        wait_all(c, *back, arrive=False)
    lanes = lax.broadcasted_iota(jnp.int32, (1, LANES), 1)
    for c in range(3):
        for copy in halos[3 * c : 3 * c + 3]:
            copy.wait_recv()
        corner = jnp.sum(
            jnp.where(lanes[:, :XPAD] == 6 * SX, corner_in[c], 0.0), axis=1, keepdims=True
        )
        row = row_in[c]
        out[c, 0:1, :] = out[c, 0:1, :] + row
        edge = jnp.broadcast_to(col_in[c], (LANES, XPAD)).T[: 6 * SX]
        first = (lax.broadcasted_iota(jnp.int32, edge.shape, 0) == 0).astype(F32)
        left = lax.broadcasted_iota(jnp.int32, edge.shape, 1) == 0
        out[c, :, :LANES] = out[c, :, :LANES] + jnp.where(left, edge + first * corner, 0.0)
    for copy in halos:
        copy.wait_send()


def local(surface_disp, proj_coords, pair_slave, pair_owner, send_list):
    wx, wy = lax.axis_size("gx"), lax.axis_size("gy")
    tiles = wx * wy
    segs = surface_disp.shape[-1]
    pairs = proj_coords.shape[-1]
    capacity = send_list.shape[-1] // tiles
    parts = -(-capacity // 8)
    slots = 8 * parts
    lists = send_list
    if slots != capacity:
        lists = lists.reshape(2, 1, tiles, capacity)
        lists = jnp.pad(lists, ((0, 0), (0, 0), (0, 0), (0, slots - capacity)), constant_values=-1)
        lists = lists.reshape(2, 1, tiles * slots)
    sizes = (wx, wy, parts, pairs, segs)
    vmem = pl.BlockSpec(memory_space=pltpu.VMEM)
    buffer = pltpu.VMEM((3, tiles, BLOCK * -(-parts // 3), LANES), F32)
    result = pl.pallas_call(
        functools.partial(kernel, sizes),
        out_shape=jax.ShapeDtypeStruct((3, 6 * SX, 6 * SY), F32),
        in_specs=[pl.BlockSpec(memory_space=pl.ANY)] * 6,
        out_specs=vmem,
        scratch_shapes=[
            pltpu.VMEM((3 * NODES, 1, segs), F32),
            pltpu.VMEM((QUADS, 2, pairs), F32),
            pltpu.VMEM((1, pairs), jnp.int32),
            pltpu.VMEM((1, pairs), jnp.int32),
            pltpu.VMEM((2, 1, tiles * slots), jnp.int32),
            pltpu.VMEM((QPAD + NPAD + QPAD, 2 * LANES), F32),
            pltpu.VMEM((3, NPAD, segs), F32),
            pltpu.VMEM((7, QPAD, pairs), F32),
            pltpu.VMEM((7, QPAD, pairs), F32),
            pltpu.VMEM((3, QPAD, pairs), F32),
            pltpu.VMEM((3, QPAD, pairs), F32),
            pltpu.VMEM((NPAD, pairs), F32),
            pltpu.VMEM((NPAD, pairs), F32),
            pltpu.VMEM((3, NPAD, segs), F32),
            pltpu.VMEM((segs // LANES, NPAD, LANES), F32),
            pltpu.VMEM((8 * SX, 7 * SY), F32),
            buffer,
            buffer,
            buffer,
            buffer,
            pltpu.VMEM((3, 1, 6 * SY), F32),
            pltpu.VMEM((3, 1, XPAD), F32),
            pltpu.VMEM((3, 1, 6 * SY), F32),
            pltpu.VMEM((3, 1, XPAD), F32),
            pltpu.VMEM((3, 1, XPAD), F32),
            pltpu.SemaphoreType.DMA((3,)),
            pltpu.SemaphoreType.DMA((3,)),
            pltpu.SemaphoreType.DMA((3,)),
            pltpu.SemaphoreType.DMA((3,)),
            pltpu.SemaphoreType.DMA((3, 3)),
            pltpu.SemaphoreType.DMA((3, 3)),
            pltpu.SemaphoreType.DMA((6,)),
        ],
        compiler_params=pltpu.CompilerParams(
            collective_id=0, has_side_effects=True, vmem_limit_bytes=60 * 1024 * 1024
        ),
    )(
        surface_disp.reshape(3 * NODES, 1, segs),
        proj_coords[0].transpose(1, 0, 2),
        pair_slave,
        pair_owner.reshape(1, pairs),
        lists,
        tables(),
    )
    return result[None]


def solution(mesh):
    return jax.shard_map(
        local,
        mesh=mesh,
        in_specs=(
            P("body", None, None, ("gx", "gy")),
            P("body", None, None, ("gx", "gy")),
            P("body", ("gx", "gy")),
            P("body", ("gx", "gy"), None),
            P(None, ("gx", "gy"), None),
        ),
        out_specs=P("body", None, "gx", "gy"),
        check_vma=False,
    )
```

```python
import functools

import jax
import jax.numpy as jnp
import numpy as np
from jax import lax
from jax.experimental import pallas as pl
from jax.experimental.pallas import tpu as pltpu
from jax.sharding import PartitionSpec as P

SX = 8
SY = 64
KAPPA = 2.0
SHEAR = 1.0
LOBATTO_POINTS = (
    -1.0,
    -0.830223896278567,
    -0.4688487934707142,
    0.0,
    0.4688487934707142,
    0.830223896278567,
    1.0,
)
GAUSS_POINTS = (
    -0.932469514203152,
    -0.6612093864662645,
    -0.2386191860831969,
    0.2386191860831969,
    0.6612093864662645,
    0.932469514203152,
)
GAUSS_WEIGHTS = (
    0.1713244923791704,
    0.3607615730481386,
    0.467913934572691,
    0.467913934572691,
    0.3607615730481386,
    0.1713244923791704,
)
MESH = pl.DeviceIdType.MESH
F32 = jnp.float32
BF16 = jnp.bfloat16
NODES = 49
NPAD = 64
LANES = 128
HEAD = 40
TAIL = NODES - HEAD
QUADS = 36
QPAD = 40
QROWS = 48
XPAD = 64
BLOCK = 10
SCALE = tuple(
    1.0 / float(np.prod([LOBATTO_POINTS[k] - LOBATTO_POINTS[m] for m in range(7) if m != k]))
    for k in range(7)
)


def tables():
    gauss = np.array(GAUSS_POINTS)
    single = np.ones((6, 7))
    for k in range(7):
        for m in range(7):
            if m != k:
                single[:, k] *= (gauss - LOBATTO_POINTS[m]) / (LOBATTO_POINTS[k] - LOBATTO_POINTS[m])
    spread = np.zeros((QPAD, NPAD), np.float32)
    spread[:QUADS, :NODES] = (single[:, None, :, None] * single[None, :, None, :]).reshape(
        QUADS, NODES
    )
    weights = np.array(GAUSS_WEIGHTS)
    quad = np.zeros((QPAD, LANES), np.float32)
    quad[:QUADS] = (weights[:, None] * weights[None, :]).reshape(QUADS, 1)
    high = spread.astype(BF16).astype(np.float32)
    low = (spread - high).astype(BF16).astype(np.float32)
    table = np.zeros((QPAD + NPAD + QPAD, 2 * LANES), np.float32)
    for i, part in enumerate((high, high, low)):
        table[:QPAD, i * NPAD : (i + 1) * NPAD] = part
        table[QPAD : QPAD + NPAD, i * QROWS : i * QROWS + QPAD] = part.T
    table[QPAD + NPAD :, :LANES] = quad
    return table


def two(x):
    high = x.astype(BF16)
    return high, (x - high.astype(F32)).astype(BF16)


def dot(a, b):
    return jnp.dot(a, b, preferred_element_type=F32)


def dot_t(a, b):
    return lax.dot_general(a, b, (((1,), (1,)), ((), ())), preferred_element_type=F32)


def dot_parts(x, b):
    rows = x.shape[0]
    both = dot(jnp.concatenate(two(x), axis=0), b)
    return both[:rows] + both[rows:]


def dot_parts_t(x, b):
    rows = x.shape[0]
    both = dot_t(jnp.concatenate(two(x), axis=0), b)
    return both[:rows] + both[rows:]


def flag(condition):
    return jnp.where(condition, 1.0, 0.0).astype(BF16)


def basis(x):
    gaps = [x - r for r in LOBATTO_POINTS]
    before = [None] * 7
    after = [None] * 7
    for k in range(1, 7):
        before[k] = gaps[0] if k == 1 else before[k - 1] * gaps[k - 1]
    for k in range(5, -1, -1):
        after[k] = gaps[6] if k == 5 else after[k + 1] * gaps[k + 1]
    out = []
    for k in range(7):
        if k == 0:
            product = after[0]
        elif k == 6:
            product = before[6]
        else:
            product = before[k] * after[k]
        out.append(product * SCALE[k])
    return out


def iota(shape, axis):
    return lax.broadcasted_iota(jnp.int32, shape, axis)


def head_mask(part):
    lane = iota((1, LANES), 1)
    return jnp.where((lane >= HEAD * part) & (lane < HEAD * (part + 1)), 1.0, 0.0)


def tail_mask(part):
    lane = iota((1, 8, LANES), 2)
    start = TAIL * (4 * part + iota((1, 8, LANES), 1) // 2)
    return jnp.where((lane >= start) & (lane < start + TAIL), 1.0, 0.0)


def pack(rows, hot, tile, send, tiles, parts, ci, held):
    first = rows[:HEAD]
    head = jnp.concatenate(
        [first, first, first, jnp.zeros((LANES - 3 * HEAD, first.shape[1]), F32)], axis=0
    )
    tails = jnp.concatenate(two(rows[HEAD : HEAD + 16]), axis=0)
    tails = dot(tile, tails).astype(BF16)
    high, low = two(head)
    gathered = dot_t(hot, jnp.concatenate([high, tails[:LANES]], axis=0)) + dot_t(
        hot, jnp.concatenate([low, tails[LANES:]], axis=0)
    )
    count = 8 * tiles
    for group in range(-(-parts // 3)):
        heads, tails = None, None
        for part in range(min(3, parts - 3 * group)):
            at = (3 * group + part) * count
            block = gathered[at : at + count, :LANES]
            block = block * head_mask(part)
            heads = block if heads is None else heads + block
            block = gathered[at : at + count, LANES:].reshape(tiles, 8, LANES)
            block = block * tail_mask(part)
            tails = block if tails is None else tails + block
        groups = -(-parts // 3)
        at = ci * groups + group
        send[:, 8 * at : 8 * at + 8, :] = heads.reshape(tiles, 8, LANES)
        at = 8 * held * groups + 2 * at
        send[:, at : at + 2, :] = (tails[:, 0:2] + tails[:, 2:4]) + (
            tails[:, 4:6] + tails[:, 6:8]
        )


def unpack(recv, fold, tiles, parts, ci, held):
    count = 8 * tiles
    firsts, lasts = [], []
    for group in range(-(-parts // 3)):
        groups = -(-parts // 3)
        at = ci * groups + group
        turned = recv[:, 8 * at : 8 * at + 8, :].reshape(count, LANES).T
        at = 8 * held * groups + 2 * at
        pair = recv[:, at : at + 2, :]
        eight = jnp.concatenate([pair] * 4, axis=1)
        for part in range(min(3, parts - 3 * group)):
            firsts.append(turned[part * HEAD : (part + 1) * HEAD])
            lasts.append((eight * tail_mask(part)).reshape(count, LANES))
    last = jnp.concatenate(lasts, axis=0)
    return jnp.concatenate(
        [jnp.concatenate(firsts, axis=1), dot_t(fold, jnp.concatenate(two(last), axis=1))], axis=0
    )


def kernel(
    sizes,
    surf_in, coords_in, slaves_in, owners_in, lists_in, table_in,
    out,
    surf, coords, slaves, owners, lists, table,
    held, lb1, lb2, value, tract, nodes, force_rows, elements, strips, pads,
    send1a, send1b, recv1a, recv1b, send2a, send2b, recv2a, recv2b, row_out, col_out, row_in, col_in, corner_in,
    ss1, rs1, ss2, rs2, hs, hr, loads,
):
    wx, wy, parts, pairs, segs = sizes
    tiles = wx * wy
    body, gx, gy = lax.axis_index("body"), lax.axis_index("gx"), lax.axis_index("gy")
    other = 1 - body
    here = gx * wy + gy
    next_x, next_y = lax.rem(gx + 1, wx), lax.rem(gy + 1, wy)
    back_x, back_y = lax.rem(gx + wx - 1, wx), lax.rem(gy + wy - 1, wy)

    operands = (
        (lists_in, lists), (surf_in, surf), (owners_in, owners),
        (slaves_in, slaves), (table_in, table), (coords_in, coords),
    )
    reads = [
        pltpu.make_async_copy(src, dst, loads.at[i]) for i, (src, dst) in enumerate(operands)
    ]
    for read in reads:
        read.start()

    def repeat(step):
        if tiles <= 16:
            for j in range(tiles):
                step(j)
        else:
            lax.fori_loop(0, tiles, lambda j, carry: (step(j), carry)[1], 0)

    barrier = pltpu.get_barrier_semaphore()

    def greet(j):
        to = lax.rem(here + j, tiles)
        pl.semaphore_signal(
            barrier, inc=1, device_id=(other, to // wy, lax.rem(to, wy)), device_id_type=MESH
        )

    repeat(greet)
    for place in ((back_x, gy), (gx, back_y), (back_x, back_y)):
        pl.semaphore_signal(barrier, inc=1, device_id=(body,) + place, device_id_type=MESH)

    row, step = iota((2 * LANES, 32), 0), iota((2 * LANES, 32), 1)
    place = row - LANES * (row // LANES)
    copy = place // TAIL
    tile = flag((place - TAIL * copy + 16 * (row // LANES) == step) & (copy < 12))
    row, step = iota((24, 2 * LANES), 1), iota((24, 2 * LANES), 0)
    place = row - LANES * (row // LANES)
    copy = place // TAIL
    fold = flag((place - TAIL * copy == step) & (copy < 12))
    row, step = iota((XPAD, 16 * SX), 0), iota((XPAD, 16 * SX), 1)
    step = step - 8 * SX * (step // (8 * SX))
    la = step // 8
    together = flag((row == 6 * la + (step - 8 * la)) & (step - 8 * la < 7))
    reads[0].wait()

    own = jnp.where(body == 0, lists[0], lists[1])
    pick = own.shape[1]
    column = jnp.broadcast_to(own, (LANES, pick)).T.reshape(tiles, parts, 8, LANES)
    column = jnp.concatenate(
        [column[:, part].reshape(8 * tiles, LANES) for part in range(parts)], axis=0
    )
    lane = lax.broadcasted_iota(jnp.int32, (pick, LANES), 1)
    list_hot = jnp.concatenate(
        [flag(column == lane + LANES * j) for j in range(segs // LANES)], axis=1
    )

    def copy_of(c, send, recv, ss, rs, to, land):
        return pltpu.make_async_remote_copy(
            src_ref=send[c].at[to],
            dst_ref=recv[c].at[land],
            send_sem=ss.at[c],
            recv_sem=rs.at[c],
            device_id=(other, to // wy, lax.rem(to, wy)),
            device_id_type=MESH,
        )

    def start_all(*where):
        half = wy // 2 + tiles
        repeat(lambda j: copy_of(*where, lax.rem(here + half - j, tiles), here).start())

    def wait_all(c, send, recv, ss, rs, arrive):
        whole, sem = (recv, rs) if arrive else (send, ss)
        pltpu.make_async_copy(whole[c], whole[c], sem.at[c]).wait()

    there = ((send1a, send1b), (recv1a, recv1b), ss1, rs1)
    back = ((send2a, send2b), (recv2a, recv2b), ss2, rs2)
    stages = ((0, 0, 2), (0, 1, 2), (1, 0, 1))

    held[...] = jnp.zeros_like(held)
    reads[1].wait()
    for c in range(3):
        held[c, :NODES, :] = surf[c * NODES : (c + 1) * NODES, 0, :]
        stage, ci, count = stages[c]
        pack(held[c], list_hot, tile, there[0][stage], tiles, parts, ci, count)
        if ci == count - 1:
            if stage == 0:
                pl.semaphore_wait(barrier, tiles + 3)
            start_all(stage, *there)

    for read in reads[2:]:
        read.wait()
    tile_row = lax.broadcasted_iota(jnp.int32, (tiles, pairs), 0)
    same = flag(tile_row == owners[...])
    earlier = flag(
        lax.broadcasted_iota(jnp.int32, (pairs, pairs), 0)
        < lax.broadcasted_iota(jnp.int32, (pairs, pairs), 1)
    )
    before = dot(same, earlier)
    rank = jnp.sum(before * same.astype(F32), axis=0, keepdims=True).astype(jnp.int32)
    part_of = rank // 8
    slot = part_of * (8 * tiles) + owners[...] * 8 + (rank - 8 * part_of)
    slot_hot = flag(lax.broadcasted_iota(jnp.int32, (8 * tiles * parts, pairs), 0) == slot)
    slave_hot = flag(lax.broadcasted_iota(jnp.int32, (segs, pairs), 0) == slaves[...])

    spread = table[:QPAD, : 3 * NPAD].astype(BF16)
    for c in range(3):
        high, low = two(dot_parts(held[c], slave_hot))
        value[c] = dot(spread, jnp.concatenate([high, low, high], axis=0))

    for axis, store in ((0, lb1), (1, lb2)):
        place = jnp.concatenate(
            [coords[:, axis, :], jnp.zeros((QPAD - QUADS, pairs), F32)], axis=0
        )
        for chunk in range(QPAD // 8):
            at = slice(8 * chunk, 8 * chunk + 8)
            for k, factor in enumerate(basis(place[at])):
                store[k, at, :] = factor

    pads[...] = jnp.zeros_like(pads)
    force_rows[...] = jnp.zeros_like(force_rows)
    sign = 1.0 - 2.0 * body.astype(F32)
    blocks = [slice(b * LANES, (b + 1) * LANES) for b in range(pairs // LANES)]

    for c in range(3):
        stage, ci, count = stages[c]
        if ci == 0:
            wait_all(stage, *there, arrive=True)
        nodes[...] = dot_parts(
            unpack(there[1][stage], fold, tiles, parts, ci, count), slot_hot
        )
        for across in blocks:
            for chunk in range(QPAD // 8):
                at = slice(8 * chunk, 8 * chunk + 8)
                second = [lb2[k, at, across] for k in range(7)]
                weight = table[QPAD + NPAD + 8 * chunk : QPAD + NPAD + 8 * chunk + 8, :LANES]
                total = None
                for k in range(7):
                    inner = None
                    for m in range(7):
                        row = 7 * k + m
                        term = second[m] * nodes[row : row + 1, across]
                        inner = term if inner is None else inner + term
                    term = lb1[k, at, across] * inner
                    total = term if total is None else total + term
                offset = total - value[c, at, across]
                if c < 2:
                    force = SHEAR * offset
                else:
                    gap = -sign * offset
                    soft = jnp.maximum(gap, 0.0) + jnp.log1p(jnp.exp(-jnp.abs(gap)))
                    force = -sign * KAPPA * soft
                tract[c, at, across] = force * weight
        for across in blocks:
            minus = -tract[c, :, across]
            for m in range(7):
                weighted = lb2[m, :, across] * minus
                for k in range(7):
                    row = 7 * k + m
                    force_rows[row : row + 1, across] = jnp.sum(
                        lb1[k, :, across] * weighted, axis=0, keepdims=True
                    )
        pack(force_rows[...], slot_hot, tile, back[0][stage], tiles, parts, ci, count)
        if ci == count - 1:
            start_all(stage, *back)

    spread_t = table[QPAD : QPAD + NPAD, : 3 * QROWS].astype(BF16)
    empty = jnp.zeros((QROWS - QPAD, pairs), F32)
    for c in range(3):
        high, low = two(jnp.concatenate([tract[c], empty], axis=0))
        slave_force = dot(spread_t, jnp.concatenate([high, low, high], axis=0))
        elements[c] = dot_parts_t(slave_force, slave_hot)

    wide = SY * 6
    source = lax.broadcasted_iota(jnp.int32, (7 * SY, wide), 0)
    target = lax.broadcasted_iota(jnp.int32, (7 * SY, wide), 1)
    step_m = source // SY
    weave = flag(target == 6 * (source - step_m * SY) + step_m)

    halos = []
    for c in range(3):
        stage, ci, count = stages[c]
        if ci == 0:
            wait_all(stage, *back, arrive=True)
        total = elements[c] + dot_parts(
            unpack(back[1][stage], fold, tiles, parts, ci, count), list_hot
        )
        for block in range(segs // LANES):
            strips[block] = total[:, block * LANES : (block + 1) * LANES]
        for m in range(7):
            for la in range(SX):
                block, lane = la * SY // LANES, la * SY % LANES
                rows = strips[block, pl.ds(m, 8, stride=7), :]
                pads[8 * la : 8 * la + 8, m * SY : (m + 1) * SY] = rows[:, lane : lane + SY]
        joined = dot(together, jnp.concatenate(two(pads[...]), axis=0))
        col_out[c] = joined[:, 7 * SY - LANES :].T[LANES - 1 :, :]
        grid = dot_parts(joined, weave)
        out[c] = grid[: 6 * SX]
        row_out[c] = grid[6 * SX : 6 * SX + 1]
        messages = [
            (row_out.at[c], row_in.at[c], (next_x, gy)),
            (col_out.at[c], col_in.at[c], (gx, next_y)),
            (col_out.at[c], corner_in.at[c], (next_x, next_y)),
        ]
        for i, (src, dst, place) in enumerate(messages):
            copy = pltpu.make_async_remote_copy(
                src_ref=src,
                dst_ref=dst,
                send_sem=hs.at[c, i],
                recv_sem=hr.at[c, i],
                device_id=(body,) + place,
                device_id_type=MESH,
            )
            copy.start()
            halos.append(copy)

    for stage in range(2):
        wait_all(stage, *there, arrive=False)
        wait_all(stage, *back, arrive=False)
    lanes = lax.broadcasted_iota(jnp.int32, (1, LANES), 1)
    for c in range(3):
        for copy in halos[3 * c : 3 * c + 3]:
            copy.wait_recv()
        corner = jnp.sum(
            jnp.where(lanes[:, :XPAD] == 6 * SX, corner_in[c], 0.0), axis=1, keepdims=True
        )
        row = row_in[c]
        out[c, 0:1, :] = out[c, 0:1, :] + row
        edge = jnp.broadcast_to(col_in[c], (LANES, XPAD)).T[: 6 * SX]
        first = (lax.broadcasted_iota(jnp.int32, edge.shape, 0) == 0).astype(F32)
        left = lax.broadcasted_iota(jnp.int32, edge.shape, 1) == 0
        out[c, :, :LANES] = out[c, :, :LANES] + jnp.where(left, edge + first * corner, 0.0)
    for copy in halos:
        copy.wait_send()


def local(surface_disp, proj_coords, pair_slave, pair_owner, send_list):
    wx, wy = lax.axis_size("gx"), lax.axis_size("gy")
    tiles = wx * wy
    segs = surface_disp.shape[-1]
    pairs = proj_coords.shape[-1]
    capacity = send_list.shape[-1] // tiles
    parts = -(-capacity // 8)
    slots = 8 * parts
    lists = send_list
    if slots != capacity:
        lists = lists.reshape(2, 1, tiles, capacity)
        lists = jnp.pad(lists, ((0, 0), (0, 0), (0, 0), (0, slots - capacity)), constant_values=-1)
        lists = lists.reshape(2, 1, tiles * slots)
    sizes = (wx, wy, parts, pairs, segs)
    vmem = pl.BlockSpec(memory_space=pltpu.VMEM)
    rows = BLOCK * -(-parts // 3)
    buffers = [pltpu.VMEM((tiles, count * rows, LANES), F32) for count in (2, 1)]
    result = pl.pallas_call(
        functools.partial(kernel, sizes),
        out_shape=jax.ShapeDtypeStruct((3, 6 * SX, 6 * SY), F32),
        in_specs=[pl.BlockSpec(memory_space=pl.ANY)] * 6,
        out_specs=vmem,
        scratch_shapes=[
            pltpu.VMEM((3 * NODES, 1, segs), F32),
            pltpu.VMEM((QUADS, 2, pairs), F32),
            pltpu.VMEM((1, pairs), jnp.int32),
            pltpu.VMEM((1, pairs), jnp.int32),
            pltpu.VMEM((2, 1, tiles * slots), jnp.int32),
            pltpu.VMEM((QPAD + NPAD + QPAD, 2 * LANES), F32),
            pltpu.VMEM((3, NPAD, segs), F32),
            pltpu.VMEM((7, QPAD, pairs), F32),
            pltpu.VMEM((7, QPAD, pairs), F32),
            pltpu.VMEM((3, QPAD, pairs), F32),
            pltpu.VMEM((3, QPAD, pairs), F32),
            pltpu.VMEM((NPAD, pairs), F32),
            pltpu.VMEM((NPAD, pairs), F32),
            pltpu.VMEM((3, NPAD, segs), F32),
            pltpu.VMEM((segs // LANES, NPAD, LANES), F32),
            pltpu.VMEM((8 * SX, 7 * SY), F32),
            *(buffers * 4),
            pltpu.VMEM((3, 1, 6 * SY), F32),
            pltpu.VMEM((3, 1, XPAD), F32),
            pltpu.VMEM((3, 1, 6 * SY), F32),
            pltpu.VMEM((3, 1, XPAD), F32),
            pltpu.VMEM((3, 1, XPAD), F32),
            pltpu.SemaphoreType.DMA((2,)),
            pltpu.SemaphoreType.DMA((2,)),
            pltpu.SemaphoreType.DMA((2,)),
            pltpu.SemaphoreType.DMA((2,)),
            pltpu.SemaphoreType.DMA((3, 3)),
            pltpu.SemaphoreType.DMA((3, 3)),
            pltpu.SemaphoreType.DMA((6,)),
        ],
        compiler_params=pltpu.CompilerParams(
            collective_id=0, has_side_effects=True, vmem_limit_bytes=60 * 1024 * 1024
        ),
    )(
        surface_disp.reshape(3 * NODES, 1, segs),
        proj_coords[0].transpose(1, 0, 2),
        pair_slave,
        pair_owner.reshape(1, pairs),
        lists,
        tables(),
    )
    return result[None]


def solution(mesh):
    return jax.shard_map(
        local,
        mesh=mesh,
        in_specs=(
            P("body", None, None, ("gx", "gy")),
            P("body", None, None, ("gx", "gy")),
            P("body", ("gx", "gy")),
            P("body", ("gx", "gy"), None),
            P(None, ("gx", "gy"), None),
        ),
        out_specs=P("body", None, "gx", "gy"),
        check_vma=False,
    )
```
